256 devices in a mesh: pop: 8 (over y, core), mp: 32 (over x, z).
Axes of the slice: x: 4, y: 4, z: 8, core: 2. Of those that a mesh axis runs over, the one named last changes fastest.
Arguments:
- tokens: bfloat16 [4096, 4096], P('pop', 'mp'), may hold values from -6 to 6
- norm_gain: float32 [4096], replicated, may hold values from 0.25 to 1.75
- gate_weight: bfloat16 [4096, 14848], P(None, 'mp'), may hold values from -0.09375 to 0.09375
- up_weight: bfloat16 [4096, 14848], P(None, 'mp'), may hold values from -0.09375 to 0.09375
- down_weight: bfloat16 [14848, 4096], P('mp'), may hold values from -0.09375 to 0.09375
- gate_left: bfloat16 [32, 4, 4096], P('pop'), may hold values from -4 to 4
- up_left: bfloat16 [32, 4, 4096], P('pop'), may hold values from -4 to 4
- down_right: bfloat16 [32, 4, 4096], P('pop'), may hold values from -4 to 4
- gate_right: bfloat16 [32, 4, 14848], P('pop', None, 'mp'), may hold values from -4 to 4
- up_right: bfloat16 [32, 4, 14848], P('pop', None, 'mp'), may hold values from -4 to 4
- down_left: bfloat16 [32, 4, 14848], P('pop', None, 'mp'), may hold values from -4 to 4
- fitness: float32 [64], P('pop'), may hold values from -15 to 15
Outputs:
- mixed: bfloat16 [4096, 4096], P('pop', 'mp')
- gate_step: bfloat16 [4096, 14848], P('pop', 'mp')
- up_step: bfloat16 [4096, 14848], P('pop', 'mp')
- down_step: bfloat16 [14848, 4096], P('mp', 'pop')
The draws below stay inside these ranges and needn't reach their ends.
All inputs are finite; a program needn't handle non-finite values.
Results may differ from the reference program's by a relative error of at most 0.02.
Values may be sent and summed in bfloat16 or wider, within the bound.
A program may use at most 128 MiB of HBM per device.

```python
import math
import jax
import jax.numpy as jnp
from jax import lax

D = 4096
FF = 14848
RANK = 4
ROWS_MEM = 64
MEMBERS = 64
PAIRS = 32
ROWS = 4096
N_MP = 32


def draw_fitness(key, part):
    key = jax.random.fold_in(key, 11)
    position = jnp.arange(MEMBERS, dtype=jnp.float32) / (MEMBERS - 1)
    noise = jnp.clip(jax.random.normal(key, (MEMBERS,), jnp.float32), -4.0, 4.0)
    return (1.0 + 2.0 * position) * noise + 3.0 * position


def strengthened(array, own_key, source, target, blocks, factor):
    owner, partner = [(jnp.arange(array.shape[axis_at]) // (array.shape[axis_at] // blocks)).reshape([-1 if axis == axis_at else 1 for axis in range(array.ndim)]) for axis_at in (source, target)]
    chosen = jax.random.permutation(own_key, blocks)[partner]
    strong = (owner == chosen) | (owner == (partner + blocks // 2) % blocks)
    return jnp.where(strong, factor * array, array)


def steps_of(own_key, shape, shards, least, largest):
    level, own = 1.0, jax.random.fold_in(own_key, 6)
    for dim, shards_of in shards:
        steps = jnp.exp(jax.random.uniform(jax.random.fold_in(own, dim), (shards_of,), jnp.float32, least / len(shards), largest / len(shards)))
        level = level * jnp.repeat(steps, shape[dim] // shards_of).reshape([-1 if axis == dim else 1 for axis in range(len(shape))])
    return level


def centred(key, extent, scale, bound, shards=(), kind=jnp.bfloat16):
    factor_of = steps_of(key, extent, shards, -0.22, 0.18) if shards else 1.0
    drawn = jax.random.normal(key, extent, jnp.float32) * scale * factor_of
    return jnp.minimum(jnp.maximum(drawn, -bound), bound).astype(kind)


def noise_with(rng, shape, scale, most, shards, heavy, held_as=jnp.bfloat16):
    array = scale * jax.random.normal(rng, shape, jnp.float32)
    if shards:
        array = array * steps_of(rng, shape, shards, -0.22, 0.18)
    return jnp.clip(strengthened(array, jax.random.fold_in(rng, 3), *heavy), -most, most).astype(held_as)


def setup_inputs(seed: int = 0) -> dict:
    keys = jax.random.split(jax.random.key(seed), 13)
    return {
        "tokens": centred(keys[0], (ROWS, D), 1.0, 6.0, ((0, 8), (1, 32))),
        "norm_gain": jnp.clip(1.0 + 0.15 * jax.random.normal(keys[1], (D,), jnp.float32), 0.25, 1.75),
        "gate_weight": centred(keys[2], (D, FF), D ** -0.5, 0.09375, ((1, 32),)),
        "up_weight": centred(keys[3], (D, FF), D ** -0.5, 0.09375, ((1, 32),)),
        "down_weight": noise_with(keys[4], (FF, D), FF ** -0.5, 0.09375, ((0, 32),), (0, 1, 32, 2.75)),
        "gate_left": centred(keys[5], (PAIRS, RANK, D), 1.0, 4.0, ((0, 8),)),
        "up_left": centred(keys[6], (PAIRS, RANK, D), 1.0, 4.0, ((0, 8),)),
        "down_right": centred(keys[7], (PAIRS, RANK, D), 1.0, 4.0, ((0, 8),)),
        "gate_right": centred(keys[8], (PAIRS, RANK, FF), 1.0, 4.0, ((0, 8), (2, 32))),
        "up_right": centred(keys[9], (PAIRS, RANK, FF), 1.0, 4.0, ((0, 8), (2, 32))),
        "down_left": centred(keys[10], (PAIRS, RANK, FF), 1.0, 4.0, ((0, 8), (2, 32))),
        "fitness": draw_fitness(jax.random.fold_in(keys[12], 71), 0),
    }


def row_weighting(rows, pairs, rank, rows_member):
    member = jnp.arange(rows, dtype=jnp.int32) // rows_member
    column_pair = jnp.arange(pairs * rank, dtype=jnp.int32) // rank
    polarity = (1 - 2 * (member % 2)).astype(jnp.float32)
    return jnp.where((member // 2)[:, None] == column_pair[None, :], polarity[:, None], jnp.float32(0.0))

def perturbed(inputs, weight, left, right, weighting, spread):
    flat_left = left.reshape(-1, left.shape[2])
    projected = lax.dot_general(inputs, flat_left, (((1,), (1,)), ((), ())), preferred_element_type=jnp.float32)
    base = jnp.dot(inputs, weight, preferred_element_type=jnp.float32)
    flat_right = right.reshape(-1, right.shape[2]).astype(jnp.float32)
    return base + jnp.dot(weighting * projected * spread, flat_right, precision=lax.Precision.HIGHEST)

def outer_sum(left, right, pair_weight):
    scaled = (left.astype(jnp.float32) * pair_weight[:, None, None]).reshape(-1, left.shape[2])
    flat_right = right.astype(jnp.float32).reshape(-1, right.shape[2])
    return lax.dot_general(scaled, flat_right, (((0,), (0,)), ((), ())), precision=lax.Precision.HIGHEST)

def down_blocks(hidden, down_weight, down_left, down_right, weighting):
    block = FF // N_MP
    spread = 0.5 / math.sqrt(FF)

    def add_block(total, index):
        start = (index * block).astype(jnp.int32)
        hidden_part = lax.dynamic_slice_in_dim(hidden, start, block, 1)
        weight_part = lax.dynamic_slice_in_dim(down_weight, start, block, 0)
        left_part = lax.dynamic_slice_in_dim(down_left, start, block, 2)
        term = perturbed(hidden_part, weight_part, left_part, down_right, weighting, spread)
        rounded = lax.optimization_barrier(term.astype(jnp.bfloat16))
        return (total + rounded.astype(jnp.float32), None)
    initial = jnp.zeros((hidden.shape[0], down_weight.shape[1]), jnp.float32)
    total, unused = lax.scan(add_block, initial, jnp.arange(N_MP, dtype=jnp.int32))
    return total

def reference(tokens, norm_gain, gate_weight, up_weight, down_weight, gate_left, up_left, down_right, gate_right, up_right, down_left, fitness):
    weighting = row_weighting(ROWS, PAIRS, RANK, ROWS_MEM)
    widened = tokens.astype(jnp.float32)
    row_scale = lax.rsqrt(lax.optimization_barrier(jnp.mean(widened * widened, axis=1, keepdims=True)) + 1e-06)
    normed = (widened * row_scale * norm_gain[None, :]).astype(jnp.bfloat16)
    spread_in = 0.5 / math.sqrt(D)
    gate = perturbed(normed, gate_weight, gate_left, gate_right, weighting, spread_in)
    up_value = perturbed(normed, up_weight, up_left, up_right, weighting, spread_in)
    hidden = (jax.nn.silu(gate) * up_value).astype(jnp.bfloat16)
    down = down_blocks(hidden, down_weight, down_left, down_right, weighting)
    mixed = (widened + down).astype(jnp.bfloat16)
    center = jnp.mean(fitness)
    spread_sq = jnp.mean((fitness - center) * (fitness - center))
    shaped = (fitness - center) * lax.rsqrt(spread_sq + 1e-05)
    pair_weight = (shaped[0::2] - shaped[1::2]) / math.sqrt(PAIRS * RANK)
    gate_step = outer_sum(gate_left, gate_right, pair_weight).astype(jnp.bfloat16)
    up_step = outer_sum(up_left, up_right, pair_weight).astype(jnp.bfloat16)
    down_step = outer_sum(down_left, down_right, pair_weight).astype(jnp.bfloat16)
    return (mixed, gate_step, up_step, down_step)
```

```python
import math

import jax
import jax.numpy as jnp
from jax import lax
from jax.experimental import pallas as pl
from jax.experimental.pallas import tpu as pltpu
from jax.sharding import PartitionSpec as P

MESH = pl.DeviceIdType.MESH
BF = jnp.bfloat16
F32 = jnp.float32

NX, NZ, NPOP = 4, 8, 8
ROWS, FB, FFB, D, FF = 512, 128, 464, 4096, 14848
NCH = 4
RC = ROWS // NCH
SLOTS = 8
OWN = 31

TREE = (
    (((0, 0), (1, 0)), ((0, 0), (3, 0)), ((0, 0), (0, 1)), ((0, 0), (0, 7))),
    (((1, 0), (2, 0)), ((0, 7), (3, 7)), ((1, 0), (1, 1)), ((0, 7), (0, 6))),
    (((0, 7), (1, 7)), ((0, 1), (3, 1)), ((0, 1), (0, 2)), ((0, 6), (0, 5))),
    (((0, 6), (1, 6)), ((0, 6), (3, 6)), ((2, 0), (2, 1)), ((0, 5), (0, 4))),
    (((0, 5), (1, 5)), ((0, 2), (3, 2)), ((1, 1), (1, 2)), ((2, 0), (2, 7))),
    (((0, 4), (1, 4)), ((3, 6), (2, 6)), ((2, 1), (2, 2)), ((0, 4), (0, 3))),
    (((1, 5), (2, 5)), ((0, 4), (3, 4)), ((1, 2), (1, 3)), ((3, 6), (3, 5))),
    (((1, 4), (2, 4)), ((0, 3), (3, 3)), ((2, 2), (2, 3))),
)
EDGES = [(s, k) + e for s, slot in enumerate(TREE) for k, e in enumerate(slot)]
OFFSET = [e[3] for e in EDGES] + [(0, 0)]
INDEX = {o: n for n, o in enumerate(OFFSET)}
PARENT = [INDEX[e[2]] for e in EDGES]
CHILDREN = [[c for c in range(31) if PARENT[c] == n] for n in range(32)]
GROUP = [list(range(4 * s, 4 * s + 4)) for s in range(SLOTS)]


def slot_of(n):
    return -1 if n == OWN else n // 4


def nt(a, b):
    return lax.dot_general(a, b, (((1,), (1,)), ((), ())), preferred_element_type=F32)


def mm(a, b):
    return jnp.dot(a, b, preferred_element_type=F32)


def kernel(
    tok_h, gain_h, wg_h, wu_h, wd_h, gl_h, ul_h, dr_h, gr_h, ur_h, dl_h, fit_h,
    mixed_ref, gs_h, us_h, ds_h,
    tok, wg, wu, wd, accg, accu, accp, sq, hid, part, rsr,
    gl, ul, dr, gr, ur, dl, lf, rf, lx, rxg, rxu, dlx,
    lsend, rsend, fsend, lrecv, rrecv, frecv, gain, gainp, fit, wcol, gsb, usb, dsb,
    wsem, lsem, osem, ag_send, ag_recv, rs_send, rs_recv, x_send, x_recv,
):
    p = lax.axis_index("pop")
    m = lax.axis_index("mp")
    x, z = m // NZ, m % NZ

    def near(k):
        if k < 2:
            return (p, ((x + (1, NX - 1)[k]) % NX) * NZ + z)
        return (p, x * NZ + (z + (1, NZ - 1)[k - 2]) % NZ)

    def source(n):
        dx, dz = OFFSET[n]
        return ((x + NX - dx) % NX) * NZ + (z + NZ - dz) % NZ

    def peer(j):
        return ((p + j) % NPOP, m)

    own = pltpu.make_async_copy(tok_h, tok.at[OWN], lsem.at[0])
    own.start()
    small = [
        pltpu.make_async_copy(a, b, lsem.at[1 + i])
        for i, (a, b) in enumerate(
            ((gl_h, gl), (ul_h, ul), (dr_h, dr), (gr_h, gr), (ur_h, ur), (dl_h, dl), (gain_h, gain), (fit_h, fit))
        )
    ]
    for c in small:
        c.start()

    bar = pltpu.get_barrier_semaphore()
    for k in range(4):
        pl.semaphore_signal(bar, inc=1, device_id=near(k), device_id_type=MESH)
    for j in range(1, NPOP):
        pl.semaphore_signal(bar, inc=1, device_id=peer(j), device_id_type=MESH)

    for s in range(SLOTS):
        for n in GROUP[s]:
            rows = pl.ds(pl.multiple_of(source(n) * FB, FB), FB)
            pltpu.make_async_copy(wg_h.at[rows], wg.at[pl.ds(n * FB, FB)], wsem.at[s]).start()
            pltpu.make_async_copy(wu_h.at[rows], wu.at[pl.ds(n * FB, FB)], wsem.at[8 + s]).start()
    for s in reversed(range(SLOTS)):
        for n in GROUP[s]:
            cols = pl.ds(pl.multiple_of(source(n) * FB, FB), FB)
            pltpu.make_async_copy(
                wd_h.at[:, cols], wd.at[pl.ds(0, FFB), pl.ds(n * FB, FB)], wsem.at[16 + s]
            ).start()

    def wait_in(s):
        rows = pl.ds(s * 512, 512)
        pltpu.make_async_copy(wg_h.at[pl.ds(0, 512)], wg.at[rows], wsem.at[s]).wait()
        pltpu.make_async_copy(wu_h.at[pl.ds(0, 512)], wu.at[rows], wsem.at[8 + s]).wait()

    def wait_down(s):
        pltpu.make_async_copy(
            wd_h.at[:, pl.ds(0, 512)], wd.at[pl.ds(0, FFB), pl.ds(s * 512, 512)], wsem.at[16 + s]
        ).wait()

    def rows_of(i):
        return pl.ds(pl.multiple_of(i * RC, RC), RC)

    def ag(n, i):
        return pltpu.make_async_remote_copy(
            src_ref=tok.at[PARENT[n]].at[rows_of(i)], dst_ref=tok.at[n].at[rows_of(i)],
            send_sem=ag_send.at[n, i], recv_sem=ag_recv.at[n, i],
            device_id=near(EDGES[n][1]), device_id_type=MESH,
        )

    def rs(n, i):
        return pltpu.make_async_remote_copy(
            src_ref=part.at[n].at[rows_of(i)], dst_ref=rsr.at[n].at[rows_of(i)],
            send_sem=rs_send.at[n, i], recv_sem=rs_recv.at[n, i],
            device_id=near(EDGES[n][1] ^ 1), device_id_type=MESH,
        )

    def exchange(j):
        to = (p + j) % NPOP
        cols = pl.ds(pl.multiple_of(to * 512, 512), 512)
        return [
            pltpu.make_async_remote_copy(
                src_ref=a, dst_ref=b, send_sem=x_send.at[j, q], recv_sem=x_recv.at[j, q],
                device_id=peer(j), device_id_type=MESH,
            )
            for q, (a, b) in enumerate(
                ((fsend, frecv.at[j]), (rsend, rrecv.at[j]), (lsend.at[:, cols], lrecv.at[j]))
            )
        ]

    own.wait()
    pl.semaphore_wait(bar, 4 + NPOP - 1)
    for i in range(NCH):
        for n in GROUP[0]:
            ag(n, i).start()

    for c in small:
        c.wait()
    fsend[...] = jnp.zeros((8, 128), F32)
    fsend[0:1, 0:8] = fit[...]
    rf[...] = jnp.zeros((16, 512), F32)
    for t, ref in enumerate((gr, ur, dl)):
        for k in range(4):
            rf[4 * k : 4 * k + 4, 0:FFB] = ref[k].astype(F32)
        rsend[16 * t : 16 * t + 16, :] = rf[...].astype(BF)
    for t, ref in enumerate((gl, ul, dr)):
        for k in range(4):
            lf[4 * k : 4 * k + 4, :] = ref[k].astype(F32)
        lsend[16 * t : 16 * t + 16, :] = lf[...].astype(BF)
    for j in range(1, NPOP):
        for c in exchange(j):
            c.start()
    frecv[0] = fsend[...]
    rrecv[0] = rsend[...]
    lrecv[0] = lsend[:, pl.ds(pl.multiple_of(p * 512, 512), 512)]

    zero16 = jnp.zeros((16, 512), BF)
    rxg[...] = jnp.concatenate([rsend[0:16, :], rsend[0:16, :], zero16, zero16], axis=0)
    rxu[...] = jnp.concatenate([zero16, zero16, rsend[16:32, :], rsend[16:32, :]], axis=0)
    dlx[...] = jnp.concatenate([zero16] * 5 + [rsend[32:48, :], rsend[32:48, :], zero16], axis=0)
    for n in range(32):
        cols = pl.ds(pl.multiple_of(source(n) * FB, FB), FB)
        to = pl.ds(n * FB, FB)
        a, b, c = lsend[0:16, cols], lsend[16:32, cols], lsend[32:48, cols]
        lx[:, to] = jnp.concatenate([a, a, b, b], axis=0)
        wd[FFB:512, to] = jnp.concatenate([c, c, jnp.zeros((16, FB), BF)], axis=0)
        gainp[n : n + 1, :] = gain[pl.ds(source(n), 1), :]
    hid[:, 384:512] = jnp.zeros((ROWS, 128), BF)

    def project(s, i):
        rows = rows_of(i)
        blocks, square = [], None
        for n in GROUP[s]:
            t = tok[n, rows, :].astype(F32)
            square = t * t if square is None else square + t * t
            blocks.append((t * gainp[n : n + 1, :]).astype(BF))
        v = jnp.concatenate(blocks, axis=1)
        at = pl.ds(s * 512, 512)
        g, u, q = mm(v, wg[at, :]), mm(v, wu[at, :]), nt(v, lx[:, s * 512 : s * 512 + 512])
        if s == 0:
            accg[rows, :], accu[rows, :], accp[rows, :], sq[rows, :] = g, u, q, square
        else:
            accg[rows, :] += g
            accu[rows, :] += u
            accp[rows, :] += q
            sq[rows, :] += square

    def weighting(i, lanes):
        row = lax.broadcasted_iota(jnp.int32, (RC, lanes), 0) + i * RC
        lane = lax.broadcasted_iota(jnp.int32, (RC, lanes), 1)
        member = row // 64
        sign = (1 - 2 * (member % 2)).astype(F32)
        return jnp.where((lane % 16) // 4 == member // 2, sign, 0.0), lane

    def split(value, first):
        high = value.astype(BF).astype(F32)
        return jnp.where(first, high, value - high).astype(BF)

    def finish(i):
        rows = rows_of(i)
        scale = lax.rsqrt(jnp.sum(sq[rows, :], axis=1, keepdims=True) * (1.0 / D) + 1e-06)
        sign, lane = weighting(i, 64)
        coef = sign * (accp[rows, :] * scale) * (0.5 / math.sqrt(D))
        coef = split(coef, lane % 32 < 16)
        gate = accg[rows, :] * scale + mm(coef, rxg[:, 0:FFB])
        up = accu[rows, :] * scale + mm(coef, rxu[:, 0:FFB])
        hid[rows, 0:FFB] = (gate / (1.0 + jnp.exp(-gate)) * up).astype(BF)
        projected = nt(hid[rows, :], dlx[...])
        sign, lane = weighting(i, 128)
        coef = sign * projected * (0.5 / math.sqrt(FF))
        coef = split(coef, lane < 96)
        tail = hid[rows, 384:512]
        inside = (lane < 80).astype(F32)
        pert = ((lane >= 80) & (lane < 112)).astype(F32)
        hid[rows, 384:512] = jnp.where(
            inside > 0, tail.astype(F32), jnp.where(pert > 0, coef.astype(F32), 0.0)
        ).astype(BF)

    def down(s, i):
        rows = rows_of(i)
        y = mm(hid[rows, :], wd[:, s * 512 : s * 512 + 512])
        for q, n in enumerate(GROUP[s]):
            part[n, rows, :] = y[:, q * FB : (q + 1) * FB].astype(BF)

    def add_children(n, i):
        rows = rows_of(i)
        if CHILDREN[n]:
            total = part[n, rows, :].astype(F32)
            for c in CHILDREN[n]:
                rs(c, i).wait_recv()
                total = total + rsr[c, rows, :].astype(F32)
            return total
        return None

    def shape_weights():
        every = frecv[:, 0, :]
        lane = lax.broadcasted_iota(jnp.int32, (8, 128), 1)
        valid = lane < 8
        center = jnp.sum(jnp.where(valid, every, 0.0)) * (1.0 / 64)
        off = jnp.where(valid, every - center, 0.0)
        var = jnp.sum(off * off) * (1.0 / 64)
        shaped = off * lax.rsqrt(jnp.broadcast_to(var + 1e-05, (8, 128)))
        wide = jnp.broadcast_to(shaped[:, None, :], (8, 16, 128)).reshape(128, 128)
        row = lax.broadcasted_iota(jnp.int32, (128, 128), 0)
        lane = lax.broadcasted_iota(jnp.int32, (128, 128), 1)
        k = (row % 16) // 4
        pick = jnp.where(lane == 2 * k, 1.0, jnp.where(lane == 2 * k + 1, -1.0, 0.0))
        col = jnp.sum(wide * pick, axis=1, keepdims=True) * (1.0 / math.sqrt(128))
        wcol[...] = jnp.broadcast_to(col, (128, 128))

    def step(t, i):
        rows = rows_of(i)
        take = pl.ds(16 * t, 16)
        if t < 2:
            left = lrecv[:, take, rows].reshape(128, 128).astype(F32) * wcol[...]
            left = left.T
            high = left.astype(BF)
            low = (left - high.astype(F32)).astype(BF)
            right = rrecv[:, take, :].reshape(128, 512)
            out = mm(jnp.concatenate([high, low], axis=1), jnp.concatenate([right, right], axis=0))
            (gsb, usb)[t][rows, :] = out[:, 0:FFB].astype(BF)
        else:
            left = rrecv[:, take, rows].reshape(128, 128).astype(F32).T.astype(BF)
            right = lrecv[:, take, :].reshape(128, 512).astype(F32) * wcol[:, 0:1]
            high = right.astype(BF)
            low = (right - high.astype(F32)).astype(BF)
            out = mm(jnp.concatenate([left, left], axis=1), jnp.concatenate([high, low], axis=0))
            dsb[rows, :] = out.astype(BF)

    outs = [
        pltpu.make_async_copy(gsb, gs_h, osem.at[0]),
        pltpu.make_async_copy(usb, us_h, osem.at[1]),
        pltpu.make_async_copy(dsb.at[pl.ds(0, FFB)], ds_h, osem.at[2]),
    ]

    for s in range(1, SLOTS):
        soon = [4 * s + k for k in range(len(TREE[s])) if slot_of(PARENT[4 * s + k]) == s - 1]
        later = [4 * s + k for k in range(len(TREE[s])) if slot_of(PARENT[4 * s + k]) < s - 1]
        for i in range(NCH):
            for n in later:
                ag(n, i).start()
        wait_in(s - 1)

        def relay(i, carry, s=s, soon=soon):
            for n in GROUP[s - 1]:
                ag(n, i).wait_recv()
            for n in soon:
                ag(n, i).start()
            project(s - 1, i)
            return carry

        lax.fori_loop(0, NCH, relay, 0)

    wait_in(SLOTS - 1)
    wait_down(SLOTS - 1)
    wait_down(SLOTS - 2)

    def turn(i, carry):
        for n in GROUP[SLOTS - 1][:3]:
            ag(n, i).wait_recv()
        project(SLOTS - 1, i)
        finish(i)
        down(SLOTS - 1, i)
        for n in GROUP[SLOTS - 1][:3]:
            rs(n, i).start()
        down(SLOTS - 2, i)
        return carry

    lax.fori_loop(0, NCH, turn, 0)

    for j in range(1, NPOP):
        for c in exchange(j):
            c.wait_recv()
    shape_weights()

    for s in reversed(range(SLOTS - 1)):
        if s > 0:
            wait_down(s - 1)

        def reduce(i, carry, s=s):
            for n in GROUP[s]:
                total = add_children(n, i)
                if total is not None:
                    part[n, rows_of(i), :] = total.astype(BF)
                rs(n, i).start()
            if s > 0:
                down(s - 1, i)
            if 3 <= s <= 5:
                step(5 - s, i)
            return carry

        lax.fori_loop(0, NCH, reduce, 0)
        if 3 <= s <= 5:
            outs[5 - s].start()

    def last(i, carry):
        rows = rows_of(i)
        total = add_children(OWN, i) + tok[OWN, rows, :].astype(F32)
        mixed_ref[rows, :] = total.astype(BF)
        return carry

    lax.fori_loop(0, NCH, last, 0)

    def drain(i, carry):
        for n in range(31):
            ag(n, i).wait_send()
            rs(n, i).wait_send()
        return carry

    lax.fori_loop(0, NCH, drain, 0)
    for j in range(1, NPOP):
        for c in exchange(j):
            c.wait_send()
    for c in outs:
        c.wait()


def per_device(tokens, norm_gain, gate_weight, up_weight, down_weight, gate_left, up_left, down_right,
               gate_right, up_right, down_left, fitness):
    vm = pltpu.VMEM
    dma = pltpu.SemaphoreType.DMA
    anywhere = pl.BlockSpec(memory_space=pl.ANY)
    return pl.pallas_call(
        kernel,
        out_shape=(
            jax.ShapeDtypeStruct((ROWS, FB), BF),
            jax.ShapeDtypeStruct((512, FFB), BF),
            jax.ShapeDtypeStruct((512, FFB), BF),
            jax.ShapeDtypeStruct((FFB, 512), BF),
        ),
        in_specs=[anywhere] * 12,
        out_specs=(pl.BlockSpec(memory_space=pltpu.VMEM), anywhere, anywhere, anywhere),
        scratch_shapes=[
            vm((32, ROWS, FB), BF),
            vm((D, FFB), BF),
            vm((D, FFB), BF),
            vm((512, D), BF),
            vm((ROWS, FFB), F32),
            vm((ROWS, FFB), F32),
            vm((ROWS, 64), F32),
            vm((ROWS, FB), F32),
            vm((ROWS, 512), BF),
            vm((32, ROWS, FB), BF),
            vm((31, ROWS, FB), BF),
            vm((4, 4, D), BF),
            vm((4, 4, D), BF),
            vm((4, 4, D), BF),
            vm((4, 4, FFB), BF),
            vm((4, 4, FFB), BF),
            vm((4, 4, FFB), BF),
            vm((16, D), F32),
            vm((16, 512), F32),
            vm((64, D), BF),
            vm((64, 512), BF),
            vm((64, 512), BF),
            vm((128, 512), BF),
            vm((48, D), BF),
            vm((48, 512), BF),
            vm((8, 128), F32),
            vm((8, 48, 512), BF),
            vm((8, 48, 512), BF),
            vm((8, 8, 128), F32),
            vm((32, FB), F32),
            vm((32, FB), F32),
            vm((1, 8), F32),
            vm((128, 128), F32),
            vm((512, FFB), BF),
            vm((512, FFB), BF),
            vm((512, 512), BF),
            dma((24,)),
            dma((9,)),
            dma((3,)),
            dma((31, NCH)),
            dma((31, NCH)),
            dma((31, NCH)),
            dma((31, NCH)),
            dma((8, 3)),
            dma((8, 3)),
        ],
        compiler_params=pltpu.CompilerParams(
            collective_id=0, has_side_effects=True, vmem_limit_bytes=56 << 20
        ),
        cost_estimate=pl.CostEstimate(flops=6_500_000_000, bytes_accessed=14_000_000, transcendentals=250_000),
        name="es_step",
    )(
        tokens, norm_gain.reshape(32, FB), gate_weight, up_weight, down_weight, gate_left, up_left, down_right,
        gate_right, up_right, down_left, fitness.reshape(1, 8),
    )


def solution(mesh):
    in_specs = (
        P("pop", "mp"),
        P(),
        P(None, "mp"),
        P(None, "mp"),
        P("mp", None),
        P("pop", None, None),
        P("pop", None, None),
        P("pop", None, None),
        P("pop", None, "mp"),
        P("pop", None, "mp"),
        P("pop", None, "mp"),
        P("pop"),
    )
    out_specs = (P("pop", "mp"), P("pop", "mp"), P("pop", "mp"), P("mp", "pop"))
    return jax.shard_map(
        per_device, mesh=mesh, in_specs=in_specs, out_specs=out_specs, check_vma=False
    )
```

```python
import math

import jax
import jax.numpy as jnp
from jax import lax
from jax.experimental import pallas as pl
from jax.experimental.pallas import tpu as pltpu
from jax.sharding import PartitionSpec as P

MESH = pl.DeviceIdType.MESH
BF = jnp.bfloat16
F32 = jnp.float32

NX, NZ, NPOP = 4, 8, 8
ROWS, FB, FFB, D, FF = 512, 128, 464, 4096, 14848
NCH = 4
RC = ROWS // NCH
SLOTS = 8
OWN = 31

TREE = (
    (((0, 0), (1, 0)), ((0, 0), (3, 0)), ((0, 0), (0, 1)), ((0, 0), (0, 7))),
    (((1, 0), (2, 0)), ((0, 7), (3, 7)), ((1, 0), (1, 1)), ((0, 7), (0, 6))),
    (((0, 7), (1, 7)), ((0, 1), (3, 1)), ((0, 1), (0, 2)), ((0, 6), (0, 5))),
    (((0, 6), (1, 6)), ((0, 6), (3, 6)), ((2, 0), (2, 1)), ((0, 5), (0, 4))),
    (((0, 5), (1, 5)), ((0, 2), (3, 2)), ((1, 1), (1, 2)), ((2, 0), (2, 7))),
    (((0, 4), (1, 4)), ((3, 6), (2, 6)), ((2, 1), (2, 2)), ((0, 4), (0, 3))),
    (((1, 5), (2, 5)), ((0, 4), (3, 4)), ((1, 2), (1, 3)), ((3, 6), (3, 5))),
    (((1, 4), (2, 4)), ((0, 3), (3, 3)), ((2, 2), (2, 3))),
)
EDGES = [(s, k) + e for s, slot in enumerate(TREE) for k, e in enumerate(slot)]
OFFSET = [e[3] for e in EDGES] + [(0, 0)]
INDEX = {o: n for n, o in enumerate(OFFSET)}
PARENT = [INDEX[e[2]] for e in EDGES]
CHILDREN = [[c for c in range(31) if PARENT[c] == n] for n in range(32)]
GROUP = [list(range(4 * s, 4 * s + 4)) for s in range(SLOTS)]


def slot_of(n):
    return -1 if n == OWN else n // 4


def nt(a, b):
    return lax.dot_general(a, b, (((1,), (1,)), ((), ())), preferred_element_type=F32)


def mm(a, b):
    return jnp.dot(a, b, preferred_element_type=F32)


def kernel(
    tok_h, gain_h, wg_h, wu_h, wd_h, gl_h, ul_h, dr_h, gr_h, ur_h, dl_h, fit_h,
    mixed_ref, gs_h, us_h, ds_h,
    tok, wg, wu, wd, accg, accu, accp, sq, hid, part, rsr,
    gl, ul, dr, gr, ur, dl, lf, rf, lx, rxg, rxu, dlx,
    lsend, rsend, fsend, lrecv, rrecv, frecv, gain, gainp, fit, wcol, gsb, usb, dsb,
    wsem, lsem, osem, ag_send, ag_recv, rs_send, rs_recv, x_send, x_recv,
):
    p = lax.axis_index("pop")
    m = lax.axis_index("mp")
    x, z = m // NZ, m % NZ

    def near(k):
        if k < 2:
            return (p, ((x + (1, NX - 1)[k]) % NX) * NZ + z)
        return (p, x * NZ + (z + (1, NZ - 1)[k - 2]) % NZ)

    def source(n):
        dx, dz = OFFSET[n]
        return ((x + NX - dx) % NX) * NZ + (z + NZ - dz) % NZ

    def peer(j):
        return ((p + j) % NPOP, m)

    own = pltpu.make_async_copy(tok_h, tok.at[OWN], lsem.at[0])
    own.start()
    small = [
        pltpu.make_async_copy(a, b, lsem.at[1 + i])
        for i, (a, b) in enumerate(
            ((gl_h, gl), (ul_h, ul), (dr_h, dr), (gr_h, gr), (ur_h, ur), (dl_h, dl), (gain_h, gain), (fit_h, fit))
        )
    ]
    for c in small:
        c.start()

    bar = pltpu.get_barrier_semaphore()
    for k in range(4):
        pl.semaphore_signal(bar, inc=1, device_id=near(k), device_id_type=MESH)
    for j in range(1, NPOP):
        pl.semaphore_signal(bar, inc=1, device_id=peer(j), device_id_type=MESH)

    for s in range(SLOTS):
        for n in GROUP[s]:
            cols = pl.ds(pl.multiple_of(source(n) * FB, FB), FB)
            to = pl.ds(n * FB, FB)
            pltpu.make_async_copy(wg_h.at[:, cols], wg.at[:, to], wsem.at[s]).start()
            pltpu.make_async_copy(wu_h.at[:, cols], wu.at[:, to], wsem.at[8 + s]).start()
    for s in reversed(range(SLOTS)):
        for n in GROUP[s]:
            cols = pl.ds(pl.multiple_of(source(n) * FB, FB), FB)
            pltpu.make_async_copy(
                wd_h.at[:, cols], wd.at[pl.ds(0, FFB), pl.ds(n * FB, FB)], wsem.at[16 + s]
            ).start()

    def wait_in(s):
        cols = pl.ds(s * 512, 512)
        pltpu.make_async_copy(wg_h.at[:, pl.ds(0, 512)], wg.at[:, cols], wsem.at[s]).wait()
        pltpu.make_async_copy(wu_h.at[:, pl.ds(0, 512)], wu.at[:, cols], wsem.at[8 + s]).wait()

    def wait_down(s):
        pltpu.make_async_copy(
            wd_h.at[:, pl.ds(0, 512)], wd.at[pl.ds(0, FFB), pl.ds(s * 512, 512)], wsem.at[16 + s]
        ).wait()

    def rows_of(i):
        return pl.ds(pl.multiple_of(i * RC, RC), RC)

    def ag(n, i):
        return pltpu.make_async_remote_copy(
            src_ref=tok.at[PARENT[n]].at[rows_of(i)], dst_ref=tok.at[n].at[rows_of(i)],
            send_sem=ag_send.at[n, i], recv_sem=ag_recv.at[n, i],
            device_id=near(EDGES[n][1]), device_id_type=MESH,
        )

    def rs(n, i):
        return pltpu.make_async_remote_copy(
            src_ref=part.at[n].at[rows_of(i)], dst_ref=rsr.at[n].at[rows_of(i)],
            send_sem=rs_send.at[n, i], recv_sem=rs_recv.at[n, i],
            device_id=near(EDGES[n][1] ^ 1), device_id_type=MESH,
        )

    def exchange(j):
        to = (p + j) % NPOP
        cols = pl.ds(pl.multiple_of(to * 512, 512), 512)
        return [
            pltpu.make_async_remote_copy(
                src_ref=a, dst_ref=b, send_sem=x_send.at[j, q], recv_sem=x_recv.at[j, q],
                device_id=peer(j), device_id_type=MESH,
            )
            for q, (a, b) in enumerate(
                ((fsend, frecv.at[j]), (rsend, rrecv.at[j]), (lsend.at[:, cols], lrecv.at[j]))
            )
        ]

    own.wait()
    pl.semaphore_wait(bar, 4 + NPOP - 1)
    for i in range(NCH):
        for n in GROUP[0]:
            ag(n, i).start()

    for c in small:
        c.wait()
    fsend[...] = jnp.zeros((8, 128), F32)
    fsend[0:1, 0:8] = fit[...]
    rf[...] = jnp.zeros((16, 512), F32)
    for t, ref in enumerate((gr, ur, dl)):
        for k in range(4):
            rf[4 * k : 4 * k + 4, 0:FFB] = ref[k].astype(F32)
        rsend[16 * t : 16 * t + 16, :] = rf[...].astype(BF)
    for t, ref in enumerate((gl, ul, dr)):
        for k in range(4):
            lf[4 * k : 4 * k + 4, :] = ref[k].astype(F32)
        lsend[16 * t : 16 * t + 16, :] = lf[...].astype(BF)
    for j in range(1, NPOP):
        for c in exchange(j):
            c.start()
    frecv[0] = fsend[...]
    rrecv[0] = rsend[...]
    lrecv[0] = lsend[:, pl.ds(pl.multiple_of(p * 512, 512), 512)]

    zero16 = jnp.zeros((16, 512), BF)
    rxg[...] = jnp.concatenate([rsend[0:16, :], rsend[0:16, :], zero16, zero16], axis=0)
    rxu[...] = jnp.concatenate([zero16, zero16, rsend[16:32, :], rsend[16:32, :]], axis=0)
    dlx[...] = jnp.concatenate([zero16] * 5 + [rsend[32:48, :], rsend[32:48, :], zero16], axis=0)
    for n in range(32):
        cols = pl.ds(pl.multiple_of(source(n) * FB, FB), FB)
        to = pl.ds(n * FB, FB)
        a, b, c = lsend[0:16, cols], lsend[16:32, cols], lsend[32:48, cols]
        lx[:, to] = jnp.concatenate([a, a, b, b], axis=0)
        wd[FFB:512, to] = jnp.concatenate([c, c, jnp.zeros((16, FB), BF)], axis=0)
        gainp[n : n + 1, :] = gain[pl.ds(source(n), 1), :]
    hid[:, 384:512] = jnp.zeros((ROWS, 128), BF)

    def project(s, i):
        rows = rows_of(i)
        blocks, square = [], None
        for n in GROUP[s]:
            t = tok[n, rows, :].astype(F32)
            square = t * t if square is None else square + t * t
            blocks.append((t * gainp[n : n + 1, :]).astype(BF))
        v = jnp.concatenate(blocks, axis=1)
        at = slice(s * 512, s * 512 + 512)
        g, u, q = nt(v, wg[:, at]), nt(v, wu[:, at]), nt(v, lx[:, at])
        if s == 0:
            accg[rows, :], accu[rows, :], accp[rows, :], sq[rows, :] = g, u, q, square
        else:
            accg[rows, :] += g
            accu[rows, :] += u
            accp[rows, :] += q
            sq[rows, :] += square

    def weighting(i, lanes):
        row = lax.broadcasted_iota(jnp.int32, (RC, lanes), 0) + i * RC
        lane = lax.broadcasted_iota(jnp.int32, (RC, lanes), 1)
        member = row // 64
        sign = (1 - 2 * (member % 2)).astype(F32)
        return jnp.where((lane % 16) // 4 == member // 2, sign, 0.0), lane

    def split(value, first):
        high = value.astype(BF).astype(F32)
        return jnp.where(first, high, value - high).astype(BF)

    def finish(i):
        rows = rows_of(i)
        scale = lax.rsqrt(jnp.sum(sq[rows, :], axis=1, keepdims=True) * (1.0 / D) + 1e-06)
        sign, lane = weighting(i, 64)
        coef = sign * (accp[rows, :] * scale) * (0.5 / math.sqrt(D))
        coef = split(coef, lane % 32 < 16)
        gate = accg[rows, :] * scale + mm(coef, rxg[:, 0:FFB])
        up = accu[rows, :] * scale + mm(coef, rxu[:, 0:FFB])
        hid[rows, 0:FFB] = (gate / (1.0 + jnp.exp(-gate)) * up).astype(BF)
        projected = nt(hid[rows, :], dlx[...])
        sign, lane = weighting(i, 128)
        coef = sign * projected * (0.5 / math.sqrt(FF))
        coef = split(coef, lane < 96)
        tail = hid[rows, 384:512]
        inside = (lane < 80).astype(F32)
        pert = ((lane >= 80) & (lane < 112)).astype(F32)
        hid[rows, 384:512] = jnp.where(
            inside > 0, tail.astype(F32), jnp.where(pert > 0, coef.astype(F32), 0.0)
        ).astype(BF)

    def down(s, i):
        rows = rows_of(i)
        y = mm(hid[rows, :], wd[:, s * 512 : s * 512 + 512])
        for q, n in enumerate(GROUP[s]):
            part[n, rows, :] = y[:, q * FB : (q + 1) * FB].astype(BF)

    def add_children(n, i):
        rows = rows_of(i)
        if CHILDREN[n]:
            total = part[n, rows, :].astype(F32)
            for c in CHILDREN[n]:
                rs(c, i).wait_recv()
                total = total + rsr[c, rows, :].astype(F32)
            return total
        return None

    def shape_weights():
        every = frecv[:, 0, :]
        lane = lax.broadcasted_iota(jnp.int32, (8, 128), 1)
        valid = lane < 8
        center = jnp.sum(jnp.where(valid, every, 0.0)) * (1.0 / 64)
        off = jnp.where(valid, every - center, 0.0)
        var = jnp.sum(off * off) * (1.0 / 64)
        shaped = off * lax.rsqrt(jnp.broadcast_to(var + 1e-05, (8, 128)))
        wide = jnp.broadcast_to(shaped[:, None, :], (8, 16, 128)).reshape(128, 128)
        row = lax.broadcasted_iota(jnp.int32, (128, 128), 0)
        lane = lax.broadcasted_iota(jnp.int32, (128, 128), 1)
        k = (row % 16) // 4
        pick = jnp.where(lane == 2 * k, 1.0, jnp.where(lane == 2 * k + 1, -1.0, 0.0))
        col = jnp.sum(wide * pick, axis=1, keepdims=True) * (1.0 / math.sqrt(128))
        wcol[...] = jnp.broadcast_to(col, (128, 128))

    def step(t, i):
        rows = rows_of(i)
        take = pl.ds(16 * t, 16)
        left = rrecv[:, take, rows].reshape(128, 128).astype(F32).T.astype(BF)
        right = lrecv[:, take, :].reshape(128, 512).astype(F32) * wcol[:, 0:1]
        high = right.astype(BF)
        low = (right - high.astype(F32)).astype(BF)
        out = mm(jnp.concatenate([left, left], axis=1), jnp.concatenate([high, low], axis=0))
        (gsb, usb, dsb)[t][rows, :] = out.astype(BF)

    outs = [
        pltpu.make_async_copy(gsb.at[pl.ds(0, FFB)], gs_h, osem.at[0]),
        pltpu.make_async_copy(usb.at[pl.ds(0, FFB)], us_h, osem.at[1]),
        pltpu.make_async_copy(dsb.at[pl.ds(0, FFB)], ds_h, osem.at[2]),
    ]

    for s in range(1, SLOTS):
        soon = [4 * s + k for k in range(len(TREE[s])) if slot_of(PARENT[4 * s + k]) == s - 1]
        later = [4 * s + k for k in range(len(TREE[s])) if slot_of(PARENT[4 * s + k]) < s - 1]
        for i in range(NCH):
            for n in later:
                ag(n, i).start()
        wait_in(s - 1)

        def relay(i, carry, s=s, soon=soon):
            for n in GROUP[s - 1]:
                ag(n, i).wait_recv()
            for n in soon:
                ag(n, i).start()
            project(s - 1, i)
            return carry

        lax.fori_loop(0, NCH, relay, 0)

    wait_in(SLOTS - 1)
    wait_down(SLOTS - 1)
    wait_down(SLOTS - 2)

    def turn(i, carry):
        for n in GROUP[SLOTS - 1][:3]:
            ag(n, i).wait_recv()
        project(SLOTS - 1, i)
        finish(i)
        down(SLOTS - 1, i)
        for n in GROUP[SLOTS - 1][:3]:
            rs(n, i).start()
        down(SLOTS - 2, i)
        return carry

    lax.fori_loop(0, NCH, turn, 0)

    for j in range(1, NPOP):
        for c in exchange(j):
            c.wait_recv()
    shape_weights()

    for s in reversed(range(SLOTS - 1)):
        if s > 0:
            wait_down(s - 1)

        def reduce(i, carry, s=s):
            for n in GROUP[s]:
                total = add_children(n, i)
                if total is not None:
                    part[n, rows_of(i), :] = total.astype(BF)
                rs(n, i).start()
            if s > 0:
                down(s - 1, i)
            if 3 <= s <= 5:
                step(5 - s, i)
            return carry

        lax.fori_loop(0, NCH, reduce, 0)
        if 3 <= s <= 5:
            outs[5 - s].start()

    def last(i, carry):
        rows = rows_of(i)
        total = add_children(OWN, i) + tok[OWN, rows, :].astype(F32)
        mixed_ref[rows, :] = total.astype(BF)
        return carry

    lax.fori_loop(0, NCH, last, 0)

    def drain(i, carry):
        for n in range(31):
            ag(n, i).wait_send()
            rs(n, i).wait_send()
        return carry

    lax.fori_loop(0, NCH, drain, 0)
    for j in range(1, NPOP):
        for c in exchange(j):
            c.wait_send()
    for c in outs:
        c.wait()


def per_device(tokens, norm_gain, gate_weight, up_weight, down_weight, gate_left, up_left, down_right,
               gate_right, up_right, down_left, fitness):
    vm = pltpu.VMEM
    dma = pltpu.SemaphoreType.DMA
    anywhere = pl.BlockSpec(memory_space=pl.ANY)
    mixed, gate_step, up_step, down_step = pl.pallas_call(
        kernel,
        out_shape=(
            jax.ShapeDtypeStruct((ROWS, FB), BF),
            jax.ShapeDtypeStruct((FFB, 512), BF),
            jax.ShapeDtypeStruct((FFB, 512), BF),
            jax.ShapeDtypeStruct((FFB, 512), BF),
        ),
        in_specs=[anywhere] * 12,
        out_specs=(pl.BlockSpec(memory_space=pltpu.VMEM), anywhere, anywhere, anywhere),
        scratch_shapes=[
            vm((32, ROWS, FB), BF),
            vm((FFB, D), BF),
            vm((FFB, D), BF),
            vm((512, D), BF),
            vm((ROWS, FFB), F32),
            vm((ROWS, FFB), F32),
            vm((ROWS, 64), F32),
            vm((ROWS, FB), F32),
            vm((ROWS, 512), BF),
            vm((32, ROWS, FB), BF),
            vm((31, ROWS, FB), BF),
            vm((4, 4, D), BF),
            vm((4, 4, D), BF),
            vm((4, 4, D), BF),
            vm((4, 4, FFB), BF),
            vm((4, 4, FFB), BF),
            vm((4, 4, FFB), BF),
            vm((16, D), F32),
            vm((16, 512), F32),
            vm((64, D), BF),
            vm((64, 512), BF),
            vm((64, 512), BF),
            vm((128, 512), BF),
            vm((48, D), BF),
            vm((48, 512), BF),
            vm((8, 128), F32),
            vm((8, 48, 512), BF),
            vm((8, 48, 512), BF),
            vm((8, 8, 128), F32),
            vm((32, FB), F32),
            vm((32, FB), F32),
            vm((1, 8), F32),
            vm((128, 128), F32),
            vm((512, 512), BF),
            vm((512, 512), BF),
            vm((512, 512), BF),
            dma((24,)),
            dma((9,)),
            dma((3,)),
            dma((31, NCH)),
            dma((31, NCH)),
            dma((31, NCH)),
            dma((31, NCH)),
            dma((8, 3)),
            dma((8, 3)),
        ],
        compiler_params=pltpu.CompilerParams(
            collective_id=0, has_side_effects=True, vmem_limit_bytes=56 << 20
        ),
        cost_estimate=pl.CostEstimate(flops=6_500_000_000, bytes_accessed=14_000_000, transcendentals=250_000),
        name="es_step",
    )(
        tokens, norm_gain.reshape(32, FB), gate_weight.T, up_weight.T, down_weight, gate_left, up_left, down_right,
        gate_right, up_right, down_left, fitness.reshape(1, 8),
    )
    mixed, gate_step, up_step, down_step = hand_over(mixed, gate_step, up_step, down_step)
    return mixed, gate_step.T, up_step.T, down_step


def move(a, b, c, d, a_out, b_out, c_out, d_out, a_mid, b_mid, c_mid, d_mid, sem):
    steps = (((a, a_mid), (a_mid, a_out)), ((b, b_mid), (b_mid, b_out)), ((c, c_mid), (c_mid, c_out)), ((d, d_mid), (d_mid, d_out)))
    first = [pltpu.make_async_copy(*one, sem.at[0, n]) for n, (one, _) in enumerate(steps)]
    second = [pltpu.make_async_copy(*two, sem.at[1, n]) for n, (_, two) in enumerate(steps)]
    for c in first:
        c.start()
    for c, d in zip(first, second):
        c.wait()
        d.start()
    for d in second:
        d.wait()


def hand_over(*arrays):
    anywhere = pl.BlockSpec(memory_space=pl.ANY)
    return pl.pallas_call(
        move,
        out_shape=tuple(jax.ShapeDtypeStruct(a.shape, a.dtype) for a in arrays),
        in_specs=[anywhere] * 4,
        out_specs=(anywhere,) * 4,
        scratch_shapes=[pltpu.VMEM(a.shape, a.dtype) for a in arrays] + [pltpu.SemaphoreType.DMA((2, 4))],
        name="hand_over",
    )(*arrays)


def solution(mesh):
    in_specs = (
        P("pop", "mp"),
        P(),
        P(None, "mp"),
        P(None, "mp"),
        P("mp", None),
        P("pop", None, None),
        P("pop", None, None),
        P("pop", None, None),
        P("pop", None, "mp"),
        P("pop", None, "mp"),
        P("pop", None, "mp"),
        P("pop"),
    )
    out_specs = (P("pop", "mp"), P("pop", "mp"), P("pop", "mp"), P("mp", "pop"))
    return jax.shard_map(
        per_device, mesh=mesh, in_specs=in_specs, out_specs=out_specs, check_vma=False
    )
```

```python
import math

import jax
import jax.numpy as jnp
from jax import lax
from jax.experimental import pallas as pl
from jax.experimental.pallas import tpu as pltpu
from jax.sharding import PartitionSpec as P

MESH = pl.DeviceIdType.MESH
BF = jnp.bfloat16
F32 = jnp.float32

NX, NZ, NPOP = 4, 8, 8
ROWS, FB, FFB, D, FF = 512, 128, 464, 4096, 14848
NCH = 4
RC = ROWS // NCH
HALF = ROWS // 2
SLOTS = 8
OWN = 31

TREE = (
    ((0, (0, 0), (1, 0)), (1, (0, 0), (3, 0)), (2, (0, 0), (0, 1)), (3, (0, 0), (0, 7))),
    ((0, (0, 1), (1, 1)), (1, (0, 7), (3, 7)), (2, (3, 0), (3, 1)), (3, (0, 7), (0, 6))),
    ((0, (0, 6), (1, 6)), (1, (3, 0), (2, 0)), (2, (0, 1), (0, 2)), (3, (1, 0), (1, 7))),
    ((0, (1, 1), (2, 1)), (1, (3, 7), (2, 7)), (2, (1, 1), (1, 2)), (3, (0, 6), (0, 5))),
    ((0, (1, 6), (2, 6)), (1, (0, 6), (3, 6)), (2, (0, 2), (0, 3)), (3, (1, 6), (1, 5))),
    ((0, (1, 5), (2, 5)), (1, (0, 5), (3, 5)), (2, (2, 1), (2, 2)), (3, (0, 5), (0, 4))),
    ((0, (0, 3), (1, 3)), (1, (0, 3), (3, 3)), (2, (3, 1), (3, 2)), (3, (1, 5), (1, 4))),
    ((1, (0, 4), (3, 4)), (2, (2, 2), (2, 3)), (3, (2, 5), (2, 4))),
)
EDGES = [(s,) + e for s, slot in enumerate(TREE) for e in slot]
OFFSET = [e[3] for e in EDGES] + [(0, 0)]
INDEX = {o: n for n, o in enumerate(OFFSET)}
PARENT = [INDEX[e[2]] for e in EDGES]
CHILDREN = [[c for c in range(31) if PARENT[c] == n] for n in range(32)]
GROUP = [list(range(4 * s, 4 * s + 4)) for s in range(SLOTS)]
EDGE_GROUP = [[n for n in g if n != OWN] for g in GROUP]

ORDER = (
    "SA0", "SB0", "SA1", "SB1", "PA0", "SA2", "SA3", "SB2", "PA1", "PB1", "SA4", "SB3", "PA2", "PA3",
    "SB4", "PB2", "SA5", "SA6", "PB3", "PA4", "SB5", "PB4", "SA7", "SB6", "PB0", "PA5", "PA6", "SB7",
    "PB5", "PA7", "FA0", "DA7", "RA7", "DA6", "PB6", "RA6", "PB7", "FB0", "DB7", "RB7", "DA5", "DB6",
    "RA5", "DB5", "DA2", "RB6", "XA0", "DA3", "DA4", "RB5", "RA4", "RA3", "DB3", "DB4", "RB4", "DB1",
    "DA1", "RA2", "RB3", "DB2", "DA0", "RB2", "TA1", "RA1", "RB1", "DB0", "RA0", "RB0", "TA0", "TA2",
    "LA0", "LB0",
)


def slot_of(n):
    return -1 if n == OWN else n // 4


def nt(a, b):
    return lax.dot_general(a, b, (((1,), (1,)), ((), ())), preferred_element_type=F32)


def mm(a, b):
    return jnp.dot(a, b, preferred_element_type=F32)


def kernel(
    tok_h, gain_h, wg_h, wu_h, wd_h, gl_h, ul_h, dr_h, gr_h, ur_h, dl_h, fit_h,
    mixed_ref, gs_h, us_h, ds_h,
    tok, wg, wu, wd, accg, accu, accp, sq, hid, part, rsr,
    gl, ul, dr, gr, ur, dl, lf, rf, lx, rxg, rxu, dlx,
    lsend, rsend, fsend, lrecv, rrecv, frecv, gain, gainp, fit, wcol, gsb, usb, dsb,
    wsem, lsem, osem, ag_send, ag_recv, rs_send, rs_recv, x_send, x_recv,
):
    p = lax.axis_index("pop")
    m = lax.axis_index("mp")
    x, z = m // NZ, m % NZ

    def near(k):
        if k < 2:
            return (p, ((x + (1, NX - 1)[k]) % NX) * NZ + z)
        return (p, x * NZ + (z + (1, NZ - 1)[k - 2]) % NZ)

    def source(n):
        dx, dz = OFFSET[n]
        return ((x + NX - dx) % NX) * NZ + (z + NZ - dz) % NZ

    def peer(j):
        return ((p + j) % NPOP, m)

    own = pltpu.make_async_copy(tok_h, tok.at[OWN], lsem.at[0])
    own.start()
    small = [
        pltpu.make_async_copy(a, b, lsem.at[1 + i])
        for i, (a, b) in enumerate(
            ((gl_h, gl), (ul_h, ul), (dr_h, dr), (gr_h, gr), (ur_h, ur), (dl_h, dl), (gain_h, gain), (fit_h, fit))
        )
    ]
    for c in small:
        c.start()

    bar = pltpu.get_barrier_semaphore()
    for k in range(4):
        pl.semaphore_signal(bar, inc=1, device_id=near(k), device_id_type=MESH)
    for j in range(1, NPOP):
        pl.semaphore_signal(bar, inc=1, device_id=peer(j), device_id_type=MESH)

    def wait_in(s):
        cols = pl.ds(s * 512, 512)
        pltpu.make_async_copy(wg_h.at[:, pl.ds(0, 512)], wg.at[:, cols], wsem.at[s]).wait()
        pltpu.make_async_copy(wu_h.at[:, pl.ds(0, 512)], wu.at[:, cols], wsem.at[8 + s]).wait()

    def wait_down(s):
        pltpu.make_async_copy(
            wd_h.at[:, pl.ds(0, 512)], wd.at[pl.ds(0, FFB), pl.ds(s * 512, 512)], wsem.at[16 + s]
        ).wait()

    def rows_of(i):
        return pl.ds(pl.multiple_of(i * RC, RC), RC)

    def ag(n, i):
        return pltpu.make_async_remote_copy(
            src_ref=(tok_h if PARENT[n] == OWN else tok.at[PARENT[n]]).at[rows_of(i)], dst_ref=tok.at[n].at[rows_of(i)],
            send_sem=ag_send, recv_sem=ag_recv.at[n, i],
            device_id=near(EDGES[n][1]), device_id_type=MESH,
        )

    def rs(n, i):
        return pltpu.make_async_remote_copy(
            src_ref=part.at[n].at[rows_of(i)], dst_ref=rsr.at[n].at[rows_of(i)],
            send_sem=rs_send, recv_sem=rs_recv.at[n, i],
            device_id=near(EDGES[n][1] ^ 1), device_id_type=MESH,
        )

    def exchange(j):
        to = (p + j) % NPOP
        cols = pl.ds(pl.multiple_of(to * 512, 512), 512)
        return [
            pltpu.make_async_remote_copy(
                src_ref=a, dst_ref=b, send_sem=x_send.at[j, q], recv_sem=x_recv.at[j, q],
                device_id=peer(j), device_id_type=MESH,
            )
            for q, (a, b) in enumerate(
                ((fsend, frecv.at[j]), (rsend, rrecv.at[j]), (lsend.at[:, cols], lrecv.at[j]))
            )
        ]

    pl.semaphore_wait(bar, 4 + NPOP - 1)
    for i in range(NCH):
        for n in EDGE_GROUP[0]:
            ag(n, i).start()

    for s in range(SLOTS):
        for n in GROUP[s]:
            cols = pl.ds(pl.multiple_of(source(n) * FB, FB), FB)
            to = pl.ds(n * FB, FB)
            pltpu.make_async_copy(wg_h.at[:, cols], wg.at[:, to], wsem.at[s]).start()
            pltpu.make_async_copy(wu_h.at[:, cols], wu.at[:, to], wsem.at[8 + s]).start()
    for s in reversed(range(SLOTS)):
        for n in GROUP[s]:
            cols = pl.ds(pl.multiple_of(source(n) * FB, FB), FB)
            pltpu.make_async_copy(
                wd_h.at[:, cols], wd.at[pl.ds(0, FFB), pl.ds(n * FB, FB)], wsem.at[16 + s]
            ).start()


    own.wait()

    for c in small:
        c.wait()
    fsend[...] = jnp.zeros((8, 128), F32)
    fsend[0:1, 0:8] = fit[...]
    rf[...] = jnp.zeros((16, 512), F32)
    for t, ref in enumerate((gr, ur, dl)):
        for k in range(4):
            rf[4 * k : 4 * k + 4, 0:FFB] = ref[k].astype(F32)
        rsend[16 * t : 16 * t + 16, :] = rf[...].astype(BF)
    for t, ref in enumerate((gl, ul, dr)):
        for k in range(4):
            lf[4 * k : 4 * k + 4, :] = ref[k].astype(F32)
        lsend[16 * t : 16 * t + 16, :] = lf[...].astype(BF)
    for j in range(1, NPOP):
        for c in exchange(j):
            c.start()
    frecv[0] = fsend[...]
    rrecv[0] = rsend[...]
    lrecv[0] = lsend[:, pl.ds(pl.multiple_of(p * 512, 512), 512)]

    zero16 = jnp.zeros((16, 512), BF)
    rxg[...] = jnp.concatenate([rsend[0:16, :], rsend[0:16, :], zero16, zero16], axis=0)
    rxu[...] = jnp.concatenate([zero16, zero16, rsend[16:32, :], rsend[16:32, :]], axis=0)
    dlx[...] = jnp.concatenate([zero16] * 5 + [rsend[32:48, :], rsend[32:48, :], zero16], axis=0)
    for n in range(32):
        cols = pl.ds(pl.multiple_of(source(n) * FB, FB), FB)
        to = pl.ds(n * FB, FB)
        a, b, c = lsend[0:16, cols], lsend[16:32, cols], lsend[32:48, cols]
        lx[:, to] = jnp.concatenate([a, a, b, b], axis=0)
        wd[FFB:512, to] = jnp.concatenate([c, c, jnp.zeros((16, FB), BF)], axis=0)
        gainp[n : n + 1, :] = gain[pl.ds(source(n), 1), :]
    hid[:, 384:512] = jnp.zeros((ROWS, 128), BF)

    def project(s, h, first):
        rows = slice(h * HALF, h * HALF + HALF)
        blocks, square = [], None
        for n in GROUP[s]:
            t = tok[n, rows, :].astype(F32)
            square = t * t if square is None else square + t * t
            blocks.append((t * gainp[n : n + 1, :]).astype(BF))
        v = jnp.concatenate(blocks, axis=1)
        at = slice(s * 512, s * 512 + 512)
        g, u, q = nt(v, wg[:, at]), nt(v, wu[:, at]), nt(v, lx[:, at])
        if first:
            accg[rows, :], accu[rows, :], accp[rows, :], sq[rows, :] = g, u, q, square
        else:
            accg[rows, :] += g
            accu[rows, :] += u
            accp[rows, :] += q
            sq[rows, :] += square

    def weighting(h, lanes):
        row = lax.broadcasted_iota(jnp.int32, (HALF, lanes), 0) + h * HALF
        lane = lax.broadcasted_iota(jnp.int32, (HALF, lanes), 1)
        member = row // 64
        sign = (1 - 2 * (member % 2)).astype(F32)
        return jnp.where((lane % 16) // 4 == member // 2, sign, 0.0), lane

    def split(value, first):
        high = value.astype(BF).astype(F32)
        return jnp.where(first, high, value - high).astype(BF)

    def finish(h, s):
        rows = slice(h * HALF, h * HALF + HALF)
        scale = lax.rsqrt(jnp.sum(sq[rows, :], axis=1, keepdims=True) * (1.0 / D) + 1e-06)
        sign, lane = weighting(h, 64)
        coef = sign * (accp[rows, :] * scale) * (0.5 / math.sqrt(D))
        coef = split(coef, lane % 32 < 16)
        gate = accg[rows, :] * scale + mm(coef, rxg[:, 0:FFB])
        up = accu[rows, :] * scale + mm(coef, rxu[:, 0:FFB])
        hid[rows, 0:FFB] = (gate / (1.0 + jnp.exp(-gate)) * up).astype(BF)
        projected = nt(hid[rows, :], dlx[...])
        sign, lane = weighting(h, 128)
        coef = sign * projected * (0.5 / math.sqrt(FF))
        coef = split(coef, lane < 96)
        tail = hid[rows, 384:512]
        inside = (lane < 80).astype(F32)
        pert = ((lane >= 80) & (lane < 112)).astype(F32)
        hid[rows, 384:512] = jnp.where(
            inside > 0, tail.astype(F32), jnp.where(pert > 0, coef.astype(F32), 0.0)
        ).astype(BF)

    def down(s, h):
        rows = slice(h * HALF, h * HALF + HALF)
        y = mm(hid[rows, :], wd[:, s * 512 : s * 512 + 512])
        for q, n in enumerate(GROUP[s]):
            part[n, rows, :] = y[:, q * FB : (q + 1) * FB].astype(BF)

    def add_children(n, i):
        rows = rows_of(i)
        if CHILDREN[n]:
            total = part[n, rows, :].astype(F32)
            for c in CHILDREN[n]:
                rs(c, i).wait_recv()
                total = total + rsr[c, rows, :].astype(F32)
            return total
        return None

    def shape_weights():
        every = frecv[:, 0, :]
        lane = lax.broadcasted_iota(jnp.int32, (8, 128), 1)
        valid = lane < 8
        center = jnp.sum(jnp.where(valid, every, 0.0)) * (1.0 / 64)
        off = jnp.where(valid, every - center, 0.0)
        var = jnp.sum(off * off) * (1.0 / 64)
        shaped = off * lax.rsqrt(jnp.broadcast_to(var + 1e-05, (8, 128)))
        wide = jnp.broadcast_to(shaped[:, None, :], (8, 16, 128)).reshape(128, 128)
        row = lax.broadcasted_iota(jnp.int32, (128, 128), 0)
        lane = lax.broadcasted_iota(jnp.int32, (128, 128), 1)
        k = (row % 16) // 4
        pick = jnp.where(lane == 2 * k, 1.0, jnp.where(lane == 2 * k + 1, -1.0, 0.0))
        col = jnp.sum(wide * pick, axis=1, keepdims=True) * (1.0 / math.sqrt(128))
        wcol[...] = jnp.broadcast_to(col, (128, 128))

    def step(t, i):
        rows = rows_of(i)
        take = pl.ds(16 * t, 16)
        left = rrecv[:, take, rows].reshape(128, 128).astype(F32).T.astype(BF)
        right = lrecv[:, take, :].reshape(128, 512).astype(F32) * wcol[:, 0:1]
        high = right.astype(BF)
        low = (right - high.astype(F32)).astype(BF)
        out = mm(jnp.concatenate([left, left], axis=1), jnp.concatenate([high, low], axis=0))
        (gsb, usb, dsb)[t][rows, :] = out.astype(BF)

    outs = [
        pltpu.make_async_copy(gsb.at[pl.ds(0, FFB)], gs_h, osem.at[0]),
        pltpu.make_async_copy(usb.at[pl.ds(0, FFB)], us_h, osem.at[1]),
        pltpu.make_async_copy(dsb.at[pl.ds(0, FFB)], ds_h, osem.at[2]),
    ]

    seen, ready_in, ready_down, begun = set(), set(), set(), set()

    def halves(h, body):
        def run(c, carry):
            body(2 * h + c)
            return carry

        lax.fori_loop(0, 2, run, 0)

    def arrive(h, blocks):
        new = [n for n in blocks if n != OWN and (h, n) not in seen]
        seen.update((h, n) for n in new)
        return new

    def send_slot(h, s):
        wait = {n: arrive(h, [PARENT[n]]) for n in EDGE_GROUP[s]}

        def body(i):
            for n in EDGE_GROUP[s]:
                for q in wait[n]:
                    ag(q, i).wait_recv()
                ag(n, i).start()

        halves(h, body)

    def project_slot(h, s):
        if s not in ready_in:
            ready_in.add(s)
            wait_in(s)
        new, first = arrive(h, GROUP[s]), h not in begun
        begun.add(h)

        def body(i):
            for n in new:
                ag(n, i).wait_recv()

        halves(h, body)
        project(s, h, first)

    def down_slot(h, s):
        if s not in ready_down:
            ready_down.add(s)
            wait_down(s)
        down(s, h)

    def reduce_slot(h, s):
        def body(i):
            for n in EDGE_GROUP[s]:
                total = add_children(n, i)
                if total is not None:
                    part[n, rows_of(i), :] = total.astype(BF)
                rs(n, i).start()

        halves(h, body)

    def last(h, s):
        def body(i):
            rows = rows_of(i)
            total = add_children(OWN, i) + tok[OWN, rows, :].astype(F32)
            mixed_ref[rows, :] = total.astype(BF)

        halves(h, body)

    def weights_ready(h, s):
        for j in range(1, NPOP):
            for c in exchange(j):
                c.wait_recv()
        shape_weights()

    def step_slot(h, t):
        def run(i, carry):
            step(t, i)
            return carry

        lax.fori_loop(0, NCH, run, 0)
        outs[t].start()

    tasks = {
        "S": send_slot, "P": project_slot, "F": finish, "D": down_slot,
        "R": reduce_slot, "L": last, "X": weights_ready, "T": step_slot,
    }
    for word in ORDER[2:]:
        tasks[word[0]]("AB".index(word[1]), int(word[2]))

    ag_all = pltpu.make_async_remote_copy(
        src_ref=tok.at[pl.ds(0, OWN)], dst_ref=tok.at[pl.ds(0, OWN)], send_sem=ag_send, recv_sem=ag_recv.at[0, 0],
        device_id=near(0), device_id_type=MESH,
    )
    rs_all = pltpu.make_async_remote_copy(
        src_ref=part.at[pl.ds(0, OWN)], dst_ref=rsr, send_sem=rs_send, recv_sem=rs_recv.at[0, 0],
        device_id=near(0), device_id_type=MESH,
    )
    ag_all.wait_send()
    rs_all.wait_send()
    for j in range(1, NPOP):
        for c in exchange(j):
            c.wait_send()
    for c in outs:
        c.wait()


def per_device(tokens, norm_gain, gate_weight, up_weight, down_weight, gate_left, up_left, down_right,
               gate_right, up_right, down_left, fitness):
    vm = pltpu.VMEM
    dma = pltpu.SemaphoreType.DMA
    anywhere = pl.BlockSpec(memory_space=pl.ANY)
    mixed, gate_step, up_step, down_step = pl.pallas_call(
        kernel,
        out_shape=(
            jax.ShapeDtypeStruct((ROWS, FB), BF),
            jax.ShapeDtypeStruct((FFB, 512), BF),
            jax.ShapeDtypeStruct((FFB, 512), BF),
            jax.ShapeDtypeStruct((FFB, 512), BF),
        ),
        in_specs=[anywhere] * 12,
        out_specs=(pl.BlockSpec(memory_space=pltpu.VMEM), anywhere, anywhere, anywhere),
        scratch_shapes=[
            vm((32, ROWS, FB), BF),
            vm((FFB, D), BF),
            vm((FFB, D), BF),
            vm((512, D), BF),
            vm((ROWS, FFB), F32),
            vm((ROWS, FFB), F32),
            vm((ROWS, 64), F32),
            vm((ROWS, FB), F32),
            vm((ROWS, 512), BF),
            vm((32, ROWS, FB), BF),
            vm((31, ROWS, FB), BF),
            vm((4, 4, D), BF),
            vm((4, 4, D), BF),
            vm((4, 4, D), BF),
            vm((4, 4, FFB), BF),
            vm((4, 4, FFB), BF),
            vm((4, 4, FFB), BF),
            vm((16, D), F32),
            vm((16, 512), F32),
            vm((64, D), BF),
            vm((64, 512), BF),
            vm((64, 512), BF),
            vm((128, 512), BF),
            vm((48, D), BF),
            vm((48, 512), BF),
            vm((8, 128), F32),
            vm((8, 48, 512), BF),
            vm((8, 48, 512), BF),
            vm((8, 8, 128), F32),
            vm((32, FB), F32),
            vm((32, FB), F32),
            vm((1, 8), F32),
            vm((128, 128), F32),
            vm((512, 512), BF),
            vm((512, 512), BF),
            vm((512, 512), BF),
            dma((24,)),
            dma((9,)),
            dma((3,)),
            dma,
            dma((31, NCH)),
            dma,
            dma((31, NCH)),
            dma((8, 3)),
            dma((8, 3)),
        ],
        compiler_params=pltpu.CompilerParams(
            collective_id=0, has_side_effects=True, vmem_limit_bytes=56 << 20
        ),
        cost_estimate=pl.CostEstimate(flops=6_500_000_000, bytes_accessed=14_000_000, transcendentals=250_000),
        name="es_step",
    )(
        tokens, norm_gain.reshape(32, FB), gate_weight.T, up_weight.T, down_weight, gate_left, up_left, down_right,
        gate_right, up_right, down_left, fitness.reshape(1, 8),
    )
    mixed, gate_step, up_step, down_step = hand_over(mixed, gate_step, up_step, down_step)
    return mixed, gate_step.T, up_step.T, down_step


def move(a, b, c, d, a_out, b_out, c_out, d_out, a_mid, b_mid, c_mid, d_mid, sem):
    steps = (((a, a_mid), (a_mid, a_out)), ((b, b_mid), (b_mid, b_out)), ((c, c_mid), (c_mid, c_out)), ((d, d_mid), (d_mid, d_out)))
    first = [pltpu.make_async_copy(*one, sem.at[0, n]) for n, (one, _) in enumerate(steps)]
    second = [pltpu.make_async_copy(*two, sem.at[1, n]) for n, (_, two) in enumerate(steps)]
    for c in first:
        c.start()
    for c, d in zip(first, second):
        c.wait()
        d.start()
    for d in second:
        d.wait()


def hand_over(*arrays):
    anywhere = pl.BlockSpec(memory_space=pl.ANY)
    return pl.pallas_call(
        move,
        out_shape=tuple(jax.ShapeDtypeStruct(a.shape, a.dtype) for a in arrays),
        in_specs=[anywhere] * 4,
        out_specs=(anywhere,) * 4,
        scratch_shapes=[pltpu.VMEM(a.shape, a.dtype) for a in arrays] + [pltpu.SemaphoreType.DMA((2, 4))],
        name="hand_over",
    )(*arrays)


def solution(mesh):
    in_specs = (
        P("pop", "mp"),
        P(),
        P(None, "mp"),
        P(None, "mp"),
        P("mp", None),
        P("pop", None, None),
        P("pop", None, None),
        P("pop", None, None),
        P("pop", None, "mp"),
        P("pop", None, "mp"),
        P("pop", None, "mp"),
        P("pop"),
    )
    out_specs = (P("pop", "mp"), P("pop", "mp"), P("pop", "mp"), P("mp", "pop"))
    return jax.shard_map(
        per_device, mesh=mesh, in_specs=in_specs, out_specs=out_specs, check_vma=False
    )
```

```python
import math

import jax
import jax.numpy as jnp
from jax import lax
from jax.experimental import pallas as pl
from jax.experimental.pallas import tpu as pltpu
from jax.sharding import PartitionSpec as P

MESH = pl.DeviceIdType.MESH
BF = jnp.bfloat16
F32 = jnp.float32

NX, NZ, NPOP = 4, 8, 8
ROWS, FB, FFB, D, FF = 512, 128, 464, 4096, 14848
NCH = 4
RC = ROWS // NCH
HALF = ROWS // 2
SLOTS = 8

TREE = (
    ((1, 0), 0, 1, 31), ((3, 0), 1, 1, 31), ((0, 1), 2, 1, 31), ((0, 7), 3, 1, 31),
    ((1, 1), 0, 1, 2), ((3, 7), 1, 1, 3), ((3, 1), 2, 1, 1), ((0, 6), 3, 1, 3),
    ((1, 6), 0, 1, 7), ((2, 0), 1, 1, 1), ((0, 2), 2, 1, 2), ((0, 5), 3, 1, 7),
    ((2, 1), 0, 1, 4), ((3, 6), 1, 1, 7), ((1, 2), 2, 1, 4), ((1, 7), 3, 1, 0),
    ((2, 6), 0, 1, 8), ((2, 7), 1, 1, 5), ((0, 3), 2, 1, 10), ((1, 5), 3, 1, 8),
    ((1, 3), 0, 1, 18), ((3, 5), 1, 1, 11), ((2, 2), 2, 1, 12), ((1, 4), 3, 1, 19),
    ((2, 5), 0, 1, 19), ((3, 3), 1, 1, 18), ((3, 2), 2, 1, 6), ((0, 4), 3, 1, 11),
    ((2, 3), 1, 1, 25), ((3, 4), 2, 1, 25), ((2, 4), 3, 1, 24),
)
OWN = 31
OFFSET = [e[0] for e in TREE] + [(0, 0)]
PARENT = [e[3] for e in TREE]
CHILDREN = [[c for c in range(OWN) if PARENT[c] == n] for n in range(32)]
GROUP = [list(range(4 * s, 4 * s + 4)) for s in range(SLOTS)]
REACH = sorted({(e[1], e[2]) for e in TREE} | {(e[1] ^ 1, e[2]) for e in TREE})

ORDER = (
    "SA3", "SA2", "SB3", "SA1", "SA0", "SB0", "SB1", "SB2", "KA0", "SA7", "SA10", "SA9", "SA4", "SB7",
    "SB10", "SA5", "SB4", "SA15", "SA6", "SB5", "PB0", "SA8", "SA11", "SB9", "SA18", "SB8", "SB6", "SA13",
    "SB11", "PA0", "SA12", "SB13", "SB18", "SA19", "SB12", "PA1", "SA14", "SB14", "SA25", "SB19", "SA20", "SA27",
    "SB15", "SA17", "PA2", "SA26", "PB1", "SA24", "SA16", "SA23", "SB25", "PB2", "SA21", "SA22", "SA28", "SA29",
    "SB24", "PA3", "SB16", "SB20", "SB26", "SA30", "SB27", "SB23", "SB17", "SB21", "PB3", "PA4", "SB28", "SB22",
    "SB29", "XA0", "SB30", "PA6", "PA5", "PA7", "FA0", "DA7", "RA30", "DA5", "RA28", "RA21", "RA22", "RA20",
    "RA29", "RA23", "DA6", "PB6", "RA27", "PB5", "DA4", "PB4", "RA16", "RA17", "RA26", "PB7", "FB0", "DB7",
    "RB30", "RB28", "RB29", "DB6", "DB0", "DB5", "DB4", "RB22", "RA24", "DB3", "RB23", "DB1", "DA3", "RA25",
    "RB26", "RB21", "RB20", "DA2", "RA11", "RA13", "RB14", "RA14", "RB27", "RB24", "DB2", "RB25", "DA0", "RB9",
    "RB16", "RA19", "RA12", "RA18", "DA1", "RB12", "RA6", "RB19", "RA15", "TA0", "RB17", "RB11", "RB15", "RA9",
    "RA8", "RB18", "RB6", "RB13", "RA5", "RB8", "RA4", "RB4", "RA10", "RB5", "RA7", "RB10", "RA1", "RB7",
    "RB1", "RA0", "RA2", "RA3", "RB0", "RB2", "RB3", "TA1", "LA0", "TA2", "LB0",
)
ROOTS = max(at for at in range(12) if ORDER[at][0] == "S" and PARENT[int(ORDER[at][2:])] == OWN)


def nt(a, b):
    return lax.dot_general(a, b, (((1,), (1,)), ((), ())), preferred_element_type=F32)


def mm(a, b):
    return jnp.dot(a, b, preferred_element_type=F32)


def kernel(
    tok_h, gain_h, wg_h, wu_h, wd_h, gl_h, ul_h, dr_h, gr_h, ur_h, dl_h, fit_h,
    mixed_ref, gs_h, us_h, ds_h,
    tok, wg, wu, wd, accg, accu, accp, sq, hid, part, rsr,
    gl, ul, dr, gr, ur, dl, lf, rf, lx, rxg, rxu, dlx,
    lsend, rsend, fsend, lrecv, rrecv, frecv, gain, gainp, fit, wcol, gsb, usb, dsb,
    wsem, lsem, osem, ag_send, ag_recv, rs_send, rs_recv, x_send, x_recv,
):
    p = lax.axis_index("pop")
    m = lax.axis_index("mp")
    x, z = m // NZ, m % NZ

    def near(k, hops):
        if k < 2:
            return (p, ((x + (hops, NX - hops)[k]) % NX) * NZ + z)
        return (p, x * NZ + (z + (hops, NZ - hops)[k - 2]) % NZ)

    def source(n):
        dx, dz = OFFSET[n]
        return ((x + NX - dx) % NX) * NZ + (z + NZ - dz) % NZ

    def peer(j):
        return ((p + j) % NPOP, m)

    own = pltpu.make_async_copy(tok_h, tok.at[OWN], lsem.at[0])
    own.start()
    small = [
        pltpu.make_async_copy(a, b, lsem.at[1 + i])
        for i, (a, b) in enumerate(
            ((gl_h, gl), (ul_h, ul), (dr_h, dr), (gr_h, gr), (ur_h, ur), (dl_h, dl), (gain_h, gain), (fit_h, fit))
        )
    ]
    for c in small:
        c.start()

    bar = pltpu.get_barrier_semaphore()
    for k, hops in REACH:
        pl.semaphore_signal(bar, inc=1, device_id=near(k, hops), device_id_type=MESH)
    for j in range(1, NPOP):
        pl.semaphore_signal(bar, inc=1, device_id=peer(j), device_id_type=MESH)

    def wait_in(s):
        cols = pl.ds(s * 512, 512)
        pltpu.make_async_copy(wg_h.at[:, pl.ds(0, 512)], wg.at[:, cols], wsem.at[s]).wait()
        pltpu.make_async_copy(wu_h.at[:, pl.ds(0, 512)], wu.at[:, cols], wsem.at[8 + s]).wait()

    def wait_down(s):
        pltpu.make_async_copy(
            wd_h.at[:, pl.ds(0, 512)], wd.at[pl.ds(0, FFB), pl.ds(s * 512, 512)], wsem.at[16 + s]
        ).wait()

    def rows_of(i):
        return pl.ds(pl.multiple_of(i * RC, RC), RC)

    def ag(n, i):
        return pltpu.make_async_remote_copy(
            src_ref=(tok_h if PARENT[n] == OWN else tok.at[PARENT[n]]).at[rows_of(i)], dst_ref=tok.at[n].at[rows_of(i)],
            send_sem=ag_send, recv_sem=ag_recv.at[n, i],
            device_id=near(TREE[n][1], TREE[n][2]), device_id_type=MESH,
        )

    def rs(n, i):
        return pltpu.make_async_remote_copy(
            src_ref=part.at[n].at[rows_of(i)], dst_ref=rsr.at[n].at[rows_of(i)],
            send_sem=rs_send, recv_sem=rs_recv.at[n, i],
            device_id=near(TREE[n][1] ^ 1, TREE[n][2]), device_id_type=MESH,
        )

    def exchange(j):
        to = (p + j) % NPOP
        cols = pl.ds(pl.multiple_of(to * 512, 512), 512)
        return [
            pltpu.make_async_remote_copy(
                src_ref=a, dst_ref=b, send_sem=x_send.at[j, q], recv_sem=x_recv.at[j, q],
                device_id=peer(j), device_id_type=MESH,
            )
            for q, (a, b) in enumerate(
                ((fsend, frecv.at[j]), (rsend, rrecv.at[j]), (lsend.at[:, cols], lrecv.at[j]))
            )
        ]

    pl.semaphore_wait(bar, len(REACH) + NPOP - 1)

    def load_weights():
        for s in range(SLOTS):
            for n in GROUP[s]:
                cols = pl.ds(pl.multiple_of(source(n) * FB, FB), FB)
                to = pl.ds(n * FB, FB)
                pltpu.make_async_copy(wg_h.at[:, cols], wg.at[:, to], wsem.at[s]).start()
                pltpu.make_async_copy(wu_h.at[:, cols], wu.at[:, to], wsem.at[8 + s]).start()
        for s in reversed(range(SLOTS)):
            for n in GROUP[s]:
                cols = pl.ds(pl.multiple_of(source(n) * FB, FB), FB)
                pltpu.make_async_copy(
                    wd_h.at[:, cols], wd.at[pl.ds(0, FFB), pl.ds(n * FB, FB)], wsem.at[16 + s]
                ).start()

    def pack(h, s):
        own.wait()

        for c in small:
            c.wait()
        fsend[...] = jnp.zeros((8, 128), F32)
        fsend[0:1, 0:8] = fit[...]
        rf[...] = jnp.zeros((16, 512), F32)
        for t, ref in enumerate((gr, ur, dl)):
            for k in range(4):
                rf[4 * k : 4 * k + 4, 0:FFB] = ref[k].astype(F32)
            rsend[16 * t : 16 * t + 16, :] = rf[...].astype(BF)
        for t, ref in enumerate((gl, ul, dr)):
            for k in range(4):
                lf[4 * k : 4 * k + 4, :] = ref[k].astype(F32)
            lsend[16 * t : 16 * t + 16, :] = lf[...].astype(BF)
        for j in range(1, NPOP):
            for c in exchange(j):
                c.start()
        frecv[0] = fsend[...]
        rrecv[0] = rsend[...]
        lrecv[0] = lsend[:, pl.ds(pl.multiple_of(p * 512, 512), 512)]

        zero16 = jnp.zeros((16, 512), BF)
        rxg[...] = jnp.concatenate([rsend[0:16, :], rsend[0:16, :], zero16, zero16], axis=0)
        rxu[...] = jnp.concatenate([zero16, zero16, rsend[16:32, :], rsend[16:32, :]], axis=0)
        dlx[...] = jnp.concatenate([zero16] * 5 + [rsend[32:48, :], rsend[32:48, :], zero16], axis=0)
        for n in range(32):
            cols = pl.ds(pl.multiple_of(source(n) * FB, FB), FB)
            to = pl.ds(n * FB, FB)
            a, b, c = lsend[0:16, cols], lsend[16:32, cols], lsend[32:48, cols]
            lx[:, to] = jnp.concatenate([a, a, b, b], axis=0)
            wd[FFB:512, to] = jnp.concatenate([c, c, jnp.zeros((16, FB), BF)], axis=0)
            gainp[n : n + 1, :] = gain[pl.ds(source(n), 1), :]
        hid[:, 384:512] = jnp.zeros((ROWS, 128), BF)

    def project(s, h, first):
        rows = slice(h * HALF, h * HALF + HALF)
        blocks, square = [], None
        for n in GROUP[s]:
            t = tok[n, rows, :].astype(F32)
            square = t * t if square is None else square + t * t
            blocks.append((t * gainp[n : n + 1, :]).astype(BF))
        v = jnp.concatenate(blocks, axis=1)
        at = slice(s * 512, s * 512 + 512)
        g, u, q = nt(v, wg[:, at]), nt(v, wu[:, at]), nt(v, lx[:, at])
        if first:
            accg[rows, :], accu[rows, :], accp[rows, :], sq[rows, :] = g, u, q, square
        else:
            accg[rows, :] += g
            accu[rows, :] += u
            accp[rows, :] += q
            sq[rows, :] += square

    def weighting(h, lanes):
        row = lax.broadcasted_iota(jnp.int32, (HALF, lanes), 0) + h * HALF
        lane = lax.broadcasted_iota(jnp.int32, (HALF, lanes), 1)
        member = row // 64
        sign = (1 - 2 * (member % 2)).astype(F32)
        return jnp.where((lane % 16) // 4 == member // 2, sign, 0.0), lane

    def split(value, first):
        high = value.astype(BF).astype(F32)
        return jnp.where(first, high, value - high).astype(BF)

    def finish(h, s):
        rows = slice(h * HALF, h * HALF + HALF)
        scale = lax.rsqrt(jnp.sum(sq[rows, :], axis=1, keepdims=True) * (1.0 / D) + 1e-06)
        sign, lane = weighting(h, 64)
        coef = sign * (accp[rows, :] * scale) * (0.5 / math.sqrt(D))
        coef = split(coef, lane % 32 < 16)
        gate = accg[rows, :] * scale + mm(coef, rxg[:, 0:FFB])
        up = accu[rows, :] * scale + mm(coef, rxu[:, 0:FFB])
        hid[rows, 0:FFB] = (gate / (1.0 + jnp.exp(-gate)) * up).astype(BF)
        projected = nt(hid[rows, :], dlx[...])
        sign, lane = weighting(h, 128)
        coef = sign * projected * (0.5 / math.sqrt(FF))
        coef = split(coef, lane < 96)
        tail = hid[rows, 384:512]
        inside = (lane < 80).astype(F32)
        pert = ((lane >= 80) & (lane < 112)).astype(F32)
        hid[rows, 384:512] = jnp.where(
            inside > 0, tail.astype(F32), jnp.where(pert > 0, coef.astype(F32), 0.0)
        ).astype(BF)

    def down(s, h):
        rows = slice(h * HALF, h * HALF + HALF)
        y = mm(hid[rows, :], wd[:, s * 512 : s * 512 + 512])
        for q, n in enumerate(GROUP[s]):
            part[n, rows, :] = y[:, q * FB : (q + 1) * FB].astype(BF)

    def add_children(n, i):
        rows = rows_of(i)
        if CHILDREN[n]:
            total = part[n, rows, :].astype(F32)
            for c in CHILDREN[n]:
                rs(c, i).wait_recv()
                total = total + rsr[c, rows, :].astype(F32)
            return total
        return None

    def shape_weights():
        every = frecv[:, 0, :]
        lane = lax.broadcasted_iota(jnp.int32, (8, 128), 1)
        valid = lane < 8
        center = jnp.sum(jnp.where(valid, every, 0.0)) * (1.0 / 64)
        off = jnp.where(valid, every - center, 0.0)
        var = jnp.sum(off * off) * (1.0 / 64)
        shaped = off * lax.rsqrt(jnp.broadcast_to(var + 1e-05, (8, 128)))
        wide = jnp.broadcast_to(shaped[:, None, :], (8, 16, 128)).reshape(128, 128)
        row = lax.broadcasted_iota(jnp.int32, (128, 128), 0)
        lane = lax.broadcasted_iota(jnp.int32, (128, 128), 1)
        k = (row % 16) // 4
        pick = jnp.where(lane == 2 * k, 1.0, jnp.where(lane == 2 * k + 1, -1.0, 0.0))
        col = jnp.sum(wide * pick, axis=1, keepdims=True) * (1.0 / math.sqrt(128))
        wcol[...] = jnp.broadcast_to(col, (128, 128))

    def step(t, i):
        rows = rows_of(i)
        take = pl.ds(16 * t, 16)
        left = rrecv[:, take, rows].reshape(128, 128).astype(F32).T.astype(BF)
        right = lrecv[:, take, :].reshape(128, 512).astype(F32) * wcol[:, 0:1]
        high = right.astype(BF)
        low = (right - high.astype(F32)).astype(BF)
        out = mm(jnp.concatenate([left, left], axis=1), jnp.concatenate([high, low], axis=0))
        (gsb, usb, dsb)[t][rows, :] = out.astype(BF)

    outs = [
        pltpu.make_async_copy(gsb.at[pl.ds(0, FFB)], gs_h, osem.at[0]),
        pltpu.make_async_copy(usb.at[pl.ds(0, FFB)], us_h, osem.at[1]),
        pltpu.make_async_copy(dsb.at[pl.ds(0, FFB)], ds_h, osem.at[2]),
    ]

    seen, ready_in, ready_down, begun = set(), set(), set(), set()

    def halves(h, body):
        def run(c, carry):
            body(2 * h + c)
            return carry

        lax.fori_loop(0, 2, run, 0)

    def arrive(h, blocks):
        new = [n for n in blocks if n != OWN and (h, n) not in seen]
        seen.update((h, n) for n in new)
        return new

    def send_on(h, n):
        new = arrive(h, [PARENT[n]])

        def body(i):
            for q in new:
                ag(q, i).wait_recv()
            ag(n, i).start()

        halves(h, body)

    def project_slot(h, s):
        if s not in ready_in:
            ready_in.add(s)
            wait_in(s)
        new, first = arrive(h, GROUP[s]), h not in begun
        begun.add(h)

        def body(i):
            for n in new:
                ag(n, i).wait_recv()

        halves(h, body)
        project(s, h, first)

    def down_slot(h, s):
        if s not in ready_down:
            ready_down.add(s)
            wait_down(s)
        down(s, h)

    def send_back(h, n):
        def body(i):
            total = add_children(n, i)
            if total is not None:
                part[n, rows_of(i), :] = total.astype(BF)
            rs(n, i).start()

        halves(h, body)

    def last(h, s):
        def body(i):
            rows = rows_of(i)
            total = add_children(OWN, i) + tok[OWN, rows, :].astype(F32)
            mixed_ref[rows, :] = total.astype(BF)

        halves(h, body)

    def weights_ready(h, s):
        for j in range(1, NPOP):
            for c in exchange(j):
                c.wait_recv()
        shape_weights()

    def step_slot(h, t):
        def run(i, carry):
            step(t, i)
            return carry

        lax.fori_loop(0, NCH, run, 0)
        outs[t].start()

    tasks = {
        "S": send_on, "P": project_slot, "F": finish, "D": down_slot,
        "R": send_back, "L": last, "X": weights_ready, "T": step_slot, "K": pack,
    }
    for at, word in enumerate(ORDER):
        tasks[word[0]]("AB".index(word[1]), int(word[2:]))
        if at == ROOTS:
            load_weights()

    ag_all = pltpu.make_async_remote_copy(
        src_ref=tok.at[pl.ds(0, OWN)], dst_ref=tok.at[pl.ds(0, OWN)], send_sem=ag_send, recv_sem=ag_recv.at[0, 0],
        device_id=near(0, 1), device_id_type=MESH,
    )
    rs_all = pltpu.make_async_remote_copy(
        src_ref=part.at[pl.ds(0, OWN)], dst_ref=rsr, send_sem=rs_send, recv_sem=rs_recv.at[0, 0],
        device_id=near(0, 1), device_id_type=MESH,
    )
    ag_all.wait_send()
    rs_all.wait_send()
    for j in range(1, NPOP):
        for c in exchange(j):
            c.wait_send()
    for c in outs:
        c.wait()


def per_device(tokens, norm_gain, gate_weight, up_weight, down_weight, gate_left, up_left, down_right,
               gate_right, up_right, down_left, fitness):
    vm = pltpu.VMEM
    dma = pltpu.SemaphoreType.DMA
    anywhere = pl.BlockSpec(memory_space=pl.ANY)
    mixed, gate_step, up_step, down_step = pl.pallas_call(
        kernel,
        out_shape=(
            pltpu.VMEM((ROWS, FB), BF),
            pltpu.VMEM((FFB, 512), BF),
            pltpu.VMEM((FFB, 512), BF),
            pltpu.VMEM((FFB, 512), BF),
        ),
        in_specs=[anywhere] * 12,
        out_specs=(pl.BlockSpec(memory_space=pltpu.VMEM),) * 4,
        scratch_shapes=[
            vm((32, ROWS, FB), BF),
            vm((FFB, D), BF),
            vm((FFB, D), BF),
            vm((512, D), BF),
            vm((ROWS, FFB), F32),
            vm((ROWS, FFB), F32),
            vm((ROWS, 64), F32),
            vm((ROWS, FB), F32),
            vm((ROWS, 512), BF),
            vm((32, ROWS, FB), BF),
            vm((31, ROWS, FB), BF),
            vm((4, 4, D), BF),
            vm((4, 4, D), BF),
            vm((4, 4, D), BF),
            vm((4, 4, FFB), BF),
            vm((4, 4, FFB), BF),
            vm((4, 4, FFB), BF),
            vm((16, D), F32),
            vm((16, 512), F32),
            vm((64, D), BF),
            vm((64, 512), BF),
            vm((64, 512), BF),
            vm((128, 512), BF),
            vm((48, D), BF),
            vm((48, 512), BF),
            vm((8, 128), F32),
            vm((8, 48, 512), BF),
            vm((8, 48, 512), BF),
            vm((8, 8, 128), F32),
            vm((32, FB), F32),
            vm((32, FB), F32),
            vm((1, 8), F32),
            vm((128, 128), F32),
            vm((512, 512), BF),
            vm((512, 512), BF),
            vm((512, 512), BF),
            dma((24,)),
            dma((9,)),
            dma((3,)),
            dma,
            dma((31, NCH)),
            dma,
            dma((31, NCH)),
            dma((8, 3)),
            dma((8, 3)),
        ],
        compiler_params=pltpu.CompilerParams(
            collective_id=0, has_side_effects=True, vmem_limit_bytes=56 << 20
        ),
        cost_estimate=pl.CostEstimate(flops=6_500_000_000, bytes_accessed=14_000_000, transcendentals=250_000),
        name="es_step",
    )(
        tokens, norm_gain.reshape(32, FB), gate_weight.T, up_weight.T, down_weight, gate_left, up_left, down_right,
        gate_right, up_right, down_left, fitness.reshape(1, 8),
    )
    mixed, gate_step, up_step, down_step = hand_over(mixed, gate_step, up_step, down_step)
    return mixed, gate_step.T, up_step.T, down_step


def move(a, b, c, d, a_out, b_out, c_out, d_out, sem):
    copies = [
        pltpu.make_async_copy(i, o, sem.at[n])
        for n, (i, o) in enumerate(((b, b_out), (c, c_out), (d, d_out), (a, a_out)))
    ]
    for c in copies:
        c.start()
    for c in copies:
        c.wait()


def hand_over(*arrays):
    anywhere = pl.BlockSpec(memory_space=pl.ANY)
    return pl.pallas_call(
        move,
        out_shape=tuple(jax.ShapeDtypeStruct(a.shape, a.dtype) for a in arrays),
        in_specs=[anywhere] * 4,
        out_specs=(anywhere,) * 4,
        scratch_shapes=[pltpu.SemaphoreType.DMA((4,))],
        compiler_params=pltpu.CompilerParams(vmem_limit_bytes=1 << 20),
        name="hand_over",
    )(*arrays)


def solution(mesh):
    in_specs = (
        P("pop", "mp"),
        P(),
        P(None, "mp"),
        P(None, "mp"),
        P("mp", None),
        P("pop", None, None),
        P("pop", None, None),
        P("pop", None, None),
        P("pop", None, "mp"),
        P("pop", None, "mp"),
        P("pop", None, "mp"),
        P("pop"),
    )
    out_specs = (P("pop", "mp"), P("pop", "mp"), P("pop", "mp"), P("mp", "pop"))
    return jax.shard_map(
        per_device, mesh=mesh, in_specs=in_specs, out_specs=out_specs, check_vma=False
    )
```

```python
import math

import jax
import jax.numpy as jnp
from jax import lax
from jax.experimental import pallas as pl
from jax.experimental.pallas import tpu as pltpu
from jax.sharding import PartitionSpec as P

MESH = pl.DeviceIdType.MESH
BF = jnp.bfloat16
F32 = jnp.float32

NX, NZ, NPOP = 4, 8, 8
ROWS, FB, FFB, D, FF = 512, 128, 464, 4096, 14848
NCH = 4
RC = ROWS // NCH
HALF = ROWS // 2
SLOTS = 8

OFFSET = (
    (3, 1), (3, 3), (2, 1), (0, 5), (2, 0), (3, 6), (3, 0), (1, 1), (3, 7), (1, 7), (1, 6), (0, 3),
    (0, 6), (1, 0), (0, 1), (0, 2), (3, 5), (3, 2), (1, 4), (2, 6), (1, 2), (0, 7), (2, 7), (1, 5),
    (0, 4), (1, 3), (2, 5), (2, 2), (3, 4), (2, 3), (2, 4),
    (0, 0),
)
GATHER = (
    (
        (2, 1, 6), (1, 1, 11), (0, 1, 7), (3, 1, 12), (1, 1, 6), (1, 1, 12), (1, 1, 31), (0, 1, 14),
        (1, 1, 21), (3, 1, 13), (0, 1, 12), (2, 1, 15), (3, 1, 21), (0, 1, 31), (2, 1, 31), (2, 1, 14),
        (1, 1, 3), (1, 1, 15), (3, 1, 23), (0, 1, 10), (2, 1, 7), (3, 1, 31), (3, 1, 4), (3, 1, 10),
        (3, 1, 3), (0, 1, 11), (0, 1, 23), (2, 1, 2), (2, 1, 1), (1, 1, 1), (3, 1, 26),
    ),
    (
        (2, 1, 6), (1, 1, 11), (0, 1, 7), (3, 1, 12), (1, 1, 6), (1, 1, 12), (1, 1, 31), (0, 1, 14),
        (1, 1, 21), (2, 1, 10), (0, 1, 12), (2, 1, 15), (3, 1, 21), (0, 1, 31), (2, 1, 31), (2, 1, 14),
        (1, 1, 3), (1, 1, 15), (3, 1, 23), (0, 1, 10), (0, 1, 15), (3, 1, 31), (3, 1, 4), (3, 1, 10),
        (2, 1, 11), (0, 1, 11), (0, 1, 23), (2, 1, 2), (2, 1, 1), (1, 1, 1), (3, 1, 26),
    ),
)
SCATTER = (
    (
        (2, 1, 6), (1, 1, 11), (0, 1, 7), (3, 1, 12), (1, 1, 6), (1, 1, 12), (1, 1, 31), (0, 1, 14),
        (1, 1, 21), (3, 1, 13), (0, 1, 12), (2, 1, 15), (3, 1, 21), (0, 1, 31), (2, 1, 31), (2, 1, 14),
        (1, 1, 3), (2, 1, 0), (3, 1, 23), (0, 1, 10), (2, 1, 7), (3, 1, 31), (0, 1, 9), (3, 1, 10),
        (3, 1, 3), (0, 1, 11), (0, 1, 23), (2, 1, 2), (2, 1, 1), (1, 1, 1), (3, 1, 26),
    ),
    (
        (1, 1, 14), (1, 1, 11), (0, 1, 7), (3, 1, 12), (1, 1, 6), (1, 1, 12), (1, 1, 31), (0, 1, 14),
        (1, 1, 21), (3, 1, 13), (0, 1, 12), (2, 1, 15), (3, 1, 21), (0, 1, 31), (2, 1, 31), (2, 1, 14),
        (1, 1, 3), (2, 1, 0), (3, 1, 23), (0, 1, 10), (2, 1, 7), (3, 1, 31), (1, 1, 8), (3, 1, 10),
        (3, 1, 3), (0, 1, 11), (0, 1, 23), (2, 1, 2), (2, 1, 1), (1, 1, 1), (3, 1, 26),
    ),
)
OWN = 31
CHILDREN = [[[c for c in range(OWN) if tree[c][2] == n] for n in range(32)] for tree in SCATTER]
GROUP = [list(range(4 * s, 4 * s + 4)) for s in range(SLOTS)]
REACH = sorted({(e[0] ^ turn, e[1]) for tree in GATHER + SCATTER for e in tree for turn in (0, 1)})

ORDER = (
    "SA21", "SA14", "SB6", "SA6", "SA13", "SB14", "SB21", "SB13", "KA0", "SA12", "SA8", "SA15", "SA7", "SB4",
    "SB12", "SB15", "SB7", "SA9", "SA4", "SB8", "SA10", "SA3", "SA11", "SB10", "SA5", "SA0", "SB3", "SB5",
    "SB11", "SA2", "PB3", "SA20", "SA23", "SB2", "SB0", "SA1", "SA25", "SA17", "SB23", "PA3", "SA24", "PA2",
    "SB9", "SA16", "SA22", "SA26", "SA27", "SA19", "SA18", "SB1", "PB1", "XA0", "SA28", "SA29", "SB26", "SB27",
    "SB17", "PA1", "SB25", "SB16", "SA30", "SB19", "PA0", "SB24", "SB22", "PA5", "SB18", "PB2", "PA6", "SB20",
    "SB29", "PB0", "SB30", "SB28", "PA4", "PA7", "FA0", "DA7", "RA30", "RA29", "DA6", "DA4", "DA1", "RA25",
    "RA28", "RA16", "RA27", "RA17", "RA24", "RA18", "PB6", "RA4", "RA19", "PB4", "DA5", "PB5", "RA22", "PB7",
    "FB0", "DB7", "RB30", "RB29", "RA26", "DB1", "DB5", "RB28", "DB4", "DB6", "RA5", "RB25", "RB27", "RB18",
    "DB0", "DA0", "RA3", "RB17", "DA2", "RA1", "RB20", "DA3", "RB16", "RB26", "RA20", "RA23", "RB19", "RB1",
    "RB24", "DB2", "RB5", "RB4", "RA2", "TA1", "RB2", "RA11", "RB23", "RA9", "RB22", "RA10", "DB3", "RB0",
    "RA8", "RB11", "RB3", "RA0", "RB9", "RB10", "RA15", "RA7", "RA12", "RB7", "RB15", "RB8", "RB12", "RA13",
    "RA6", "RB13", "RA14", "RA21", "RB6", "RB14", "RB21", "TA2", "TA0", "LA0", "LB0",
)
ROOTS = max(at for at in range(12) if ORDER[at][0] == "S" and GATHER["AB".index(ORDER[at][1])][int(ORDER[at][2:])][2] == OWN)


def nt(a, b):
    return lax.dot_general(a, b, (((1,), (1,)), ((), ())), preferred_element_type=F32)


def mm(a, b):
    return jnp.dot(a, b, preferred_element_type=F32)


def kernel(
    tok_h, gain_h, wg_h, wu_h, wd_h, gl_h, ul_h, dr_h, gr_h, ur_h, dl_h, fit_h,
    mixed_ref, gs_h, us_h, ds_h,
    tok, wg, wu, wd, accg, accu, accp, sq, hid, part, rsr,
    gl, ul, dr, gr, ur, dl, lf, rf, lx, rxg, rxu, dlx,
    lsend, rsend, fsend, lrecv, rrecv, frecv, gain, gainp, fit, wcol, gsb, usb, dsb,
    wsem, lsem, osem, ag_send, ag_recv, rs_send, rs_recv, x_send, x_recv,
):
    p = lax.axis_index("pop")
    m = lax.axis_index("mp")
    x, z = m // NZ, m % NZ

    def near(k, hops):
        if k < 2:
            return (p, ((x + (hops, NX - hops)[k]) % NX) * NZ + z)
        return (p, x * NZ + (z + (hops, NZ - hops)[k - 2]) % NZ)

    def source(n):
        dx, dz = OFFSET[n]
        return ((x + NX - dx) % NX) * NZ + (z + NZ - dz) % NZ

    def peer(j):
        return ((p + j) % NPOP, m)

    own = pltpu.make_async_copy(tok_h, tok.at[OWN], lsem.at[0])
    own.start()
    small = [
        pltpu.make_async_copy(a, b, lsem.at[1 + i])
        for i, (a, b) in enumerate(
            ((gl_h, gl), (ul_h, ul), (dr_h, dr), (gr_h, gr), (ur_h, ur), (dl_h, dl), (gain_h, gain), (fit_h, fit))
        )
    ]
    for c in small:
        c.start()

    bar = pltpu.get_barrier_semaphore()
    for k, hops in REACH:
        pl.semaphore_signal(bar, inc=1, device_id=near(k, hops), device_id_type=MESH)
    for j in range(1, NPOP):
        pl.semaphore_signal(bar, inc=1, device_id=peer(j), device_id_type=MESH)

    def wait_in(s):
        cols = pl.ds(s * 512, 512)
        pltpu.make_async_copy(wg_h.at[:, pl.ds(0, 512)], wg.at[:, cols], wsem.at[s]).wait()
        pltpu.make_async_copy(wu_h.at[:, pl.ds(0, 512)], wu.at[:, cols], wsem.at[8 + s]).wait()

    def wait_down(s):
        pltpu.make_async_copy(
            wd_h.at[:, pl.ds(0, 512)], wd.at[pl.ds(0, FFB), pl.ds(s * 512, 512)], wsem.at[16 + s]
        ).wait()

    def rows_of(i):
        return pl.ds(pl.multiple_of(i * RC, RC), RC)

    def ag(h, n, i):
        k, hops, parent = GATHER[h][n]
        return pltpu.make_async_remote_copy(
            src_ref=(tok_h if parent == OWN else tok.at[parent]).at[rows_of(i)], dst_ref=tok.at[n].at[rows_of(i)],
            send_sem=ag_send, recv_sem=ag_recv.at[n, i],
            device_id=near(k, hops), device_id_type=MESH,
        )

    def rs(h, n, i):
        k, hops, _ = SCATTER[h][n]
        return pltpu.make_async_remote_copy(
            src_ref=part.at[n].at[rows_of(i)], dst_ref=rsr.at[n].at[rows_of(i)],
            send_sem=rs_send, recv_sem=rs_recv.at[n, i],
            device_id=near(k ^ 1, hops), device_id_type=MESH,
        )

    def exchange(j):
        to = (p + j) % NPOP
        cols = pl.ds(pl.multiple_of(to * 512, 512), 512)
        return [
            pltpu.make_async_remote_copy(
                src_ref=a, dst_ref=b, send_sem=x_send.at[j, q], recv_sem=x_recv.at[j, q],
                device_id=peer(j), device_id_type=MESH,
            )
            for q, (a, b) in enumerate(
                ((fsend, frecv.at[j]), (rsend, rrecv.at[j]), (lsend.at[:, cols], lrecv.at[j]))
            )
        ]

    pl.semaphore_wait(bar, len(REACH) + NPOP - 1)

    def load_weights():
        for s in range(SLOTS):
            for n in GROUP[s]:
                cols = pl.ds(pl.multiple_of(source(n) * FB, FB), FB)
                to = pl.ds(n * FB, FB)
                pltpu.make_async_copy(wg_h.at[:, cols], wg.at[:, to], wsem.at[s]).start()
                pltpu.make_async_copy(wu_h.at[:, cols], wu.at[:, to], wsem.at[8 + s]).start()
        for s in reversed(range(SLOTS)):
            for n in GROUP[s]:
                cols = pl.ds(pl.multiple_of(source(n) * FB, FB), FB)
                pltpu.make_async_copy(
                    wd_h.at[:, cols], wd.at[pl.ds(0, FFB), pl.ds(n * FB, FB)], wsem.at[16 + s]
                ).start()

    def pack(h, s):
        own.wait()

        for c in small:
            c.wait()
        fsend[...] = jnp.zeros((8, 128), F32)
        fsend[0:1, 0:8] = fit[...]
        rf[...] = jnp.zeros((16, 512), F32)
        for t, ref in enumerate((gr, ur, dl)):
            for k in range(4):
                rf[4 * k : 4 * k + 4, 0:FFB] = ref[k].astype(F32)
            rsend[16 * t : 16 * t + 16, :] = rf[...].astype(BF)
        for t, ref in enumerate((gl, ul, dr)):
            for k in range(4):
                lf[4 * k : 4 * k + 4, :] = ref[k].astype(F32)
            lsend[16 * t : 16 * t + 16, :] = lf[...].astype(BF)
        for j in range(1, NPOP):
            for c in exchange(j):
                c.start()
        frecv[0] = fsend[...]
        rrecv[0] = rsend[...]
        lrecv[0] = lsend[:, pl.ds(pl.multiple_of(p * 512, 512), 512)]

        zero16 = jnp.zeros((16, 512), BF)
        rxg[...] = jnp.concatenate([rsend[0:16, :], rsend[0:16, :], zero16, zero16], axis=0)
        rxu[...] = jnp.concatenate([zero16, zero16, rsend[16:32, :], rsend[16:32, :]], axis=0)
        dlx[...] = jnp.concatenate([zero16] * 5 + [rsend[32:48, :], rsend[32:48, :], zero16], axis=0)
        for n in range(32):
            cols = pl.ds(pl.multiple_of(source(n) * FB, FB), FB)
            to = pl.ds(n * FB, FB)
            a, b, c = lsend[0:16, cols], lsend[16:32, cols], lsend[32:48, cols]
            lx[:, to] = jnp.concatenate([a, a, b, b], axis=0)
            wd[FFB:512, to] = jnp.concatenate([c, c, jnp.zeros((16, FB), BF)], axis=0)
            gainp[n : n + 1, :] = gain[pl.ds(source(n), 1), :]
        hid[:, 384:512] = jnp.zeros((ROWS, 128), BF)

    def project(s, h, first):
        rows = slice(h * HALF, h * HALF + HALF)
        blocks, square = [], None
        for n in GROUP[s]:
            t = tok[n, rows, :].astype(F32)
            square = t * t if square is None else square + t * t
            blocks.append((t * gainp[n : n + 1, :]).astype(BF))
        v = jnp.concatenate(blocks, axis=1)
        at = slice(s * 512, s * 512 + 512)
        g, u, q = nt(v, wg[:, at]), nt(v, wu[:, at]), nt(v, lx[:, at])
        if first:
            accg[rows, :], accu[rows, :], accp[rows, :], sq[rows, :] = g, u, q, square
        else:
            accg[rows, :] += g
            accu[rows, :] += u
            accp[rows, :] += q
            sq[rows, :] += square

    def weighting(h, lanes):
        row = lax.broadcasted_iota(jnp.int32, (HALF, lanes), 0) + h * HALF
        lane = lax.broadcasted_iota(jnp.int32, (HALF, lanes), 1)
        member = row // 64
        sign = (1 - 2 * (member % 2)).astype(F32)
        return jnp.where((lane % 16) // 4 == member // 2, sign, 0.0), lane

    def split(value, first):
        high = value.astype(BF).astype(F32)
        return jnp.where(first, high, value - high).astype(BF)

    def finish(h, s):
        rows = slice(h * HALF, h * HALF + HALF)
        scale = lax.rsqrt(jnp.sum(sq[rows, :], axis=1, keepdims=True) * (1.0 / D) + 1e-06)
        sign, lane = weighting(h, 64)
        coef = sign * (accp[rows, :] * scale) * (0.5 / math.sqrt(D))
        coef = split(coef, lane % 32 < 16)
        gate = accg[rows, :] * scale + mm(coef, rxg[:, 0:FFB])
        up = accu[rows, :] * scale + mm(coef, rxu[:, 0:FFB])
        hid[rows, 0:FFB] = (gate / (1.0 + jnp.exp(-gate)) * up).astype(BF)
        projected = nt(hid[rows, :], dlx[...])
        sign, lane = weighting(h, 128)
        coef = sign * projected * (0.5 / math.sqrt(FF))
        coef = split(coef, lane < 96)
        tail = hid[rows, 384:512]
        inside = (lane < 80).astype(F32)
        pert = ((lane >= 80) & (lane < 112)).astype(F32)
        hid[rows, 384:512] = jnp.where(
            inside > 0, tail.astype(F32), jnp.where(pert > 0, coef.astype(F32), 0.0)
        ).astype(BF)

    def down(s, h):
        rows = slice(h * HALF, h * HALF + HALF)
        y = mm(hid[rows, :], wd[:, s * 512 : s * 512 + 512])
        for q, n in enumerate(GROUP[s]):
            part[n, rows, :] = y[:, q * FB : (q + 1) * FB].astype(BF)

    def add_children(h, n, i):
        rows = rows_of(i)
        if CHILDREN[h][n]:
            total = part[n, rows, :].astype(F32)
            for c in CHILDREN[h][n]:
                rs(h, c, i).wait_recv()
                total = total + rsr[c, rows, :].astype(F32)
            return total
        return None

    def shape_weights():
        every = frecv[:, 0, :]
        lane = lax.broadcasted_iota(jnp.int32, (8, 128), 1)
        valid = lane < 8
        center = jnp.sum(jnp.where(valid, every, 0.0)) * (1.0 / 64)
        off = jnp.where(valid, every - center, 0.0)
        var = jnp.sum(off * off) * (1.0 / 64)
        shaped = off * lax.rsqrt(jnp.broadcast_to(var + 1e-05, (8, 128)))
        wide = jnp.broadcast_to(shaped[:, None, :], (8, 16, 128)).reshape(128, 128)
        row = lax.broadcasted_iota(jnp.int32, (128, 128), 0)
        lane = lax.broadcasted_iota(jnp.int32, (128, 128), 1)
        k = (row % 16) // 4
        pick = jnp.where(lane == 2 * k, 1.0, jnp.where(lane == 2 * k + 1, -1.0, 0.0))
        col = jnp.sum(wide * pick, axis=1, keepdims=True) * (1.0 / math.sqrt(128))
        wcol[...] = jnp.broadcast_to(col, (128, 128))

    def step(t):
        take = pl.ds(16 * t, 16)
        left = rrecv[:, take, :].reshape(128, 512).T
        right = lrecv[:, take, :].reshape(128, 512).astype(F32) * jnp.concatenate([wcol[...]] * 4, axis=1)
        high = right.astype(BF)
        low = (right - high.astype(F32)).astype(BF)
        out = mm(jnp.concatenate([left, left], axis=1), jnp.concatenate([high, low], axis=0))
        (gsb, usb, dsb)[t][...] = out.astype(BF)

    outs = [
        pltpu.make_async_copy(gsb.at[pl.ds(0, FFB)], gs_h, osem.at[0]),
        pltpu.make_async_copy(usb.at[pl.ds(0, FFB)], us_h, osem.at[1]),
        pltpu.make_async_copy(dsb.at[pl.ds(0, FFB)], ds_h, osem.at[2]),
    ]

    seen, ready_in, ready_down, begun = set(), set(), set(), set()

    def halves(h, body):
        def run(c, carry):
            body(2 * h + c)
            return carry

        lax.fori_loop(0, 2, run, 0)

    def arrive(h, blocks):
        new = [n for n in blocks if n != OWN and (h, n) not in seen]
        seen.update((h, n) for n in new)
        return new

    def send_on(h, n):
        new = arrive(h, [GATHER[h][n][2]])

        def body(i):
            for q in new:
                ag(h, q, i).wait_recv()
            ag(h, n, i).start()

        halves(h, body)

    def project_slot(h, s):
        if s not in ready_in:
            ready_in.add(s)
            wait_in(s)
        new, first = arrive(h, GROUP[s]), h not in begun
        begun.add(h)

        def body(i):
            for n in new:
                ag(h, n, i).wait_recv()

        halves(h, body)
        project(s, h, first)

    def down_slot(h, s):
        if s not in ready_down:
            ready_down.add(s)
            wait_down(s)
        down(s, h)

    def send_back(h, n):
        def body(i):
            total = add_children(h, n, i)
            if total is not None:
                part[n, rows_of(i), :] = total.astype(BF)
            rs(h, n, i).start()

        halves(h, body)

    def last(h, s):
        def body(i):
            rows = rows_of(i)
            total = add_children(h, OWN, i) + tok[OWN, rows, :].astype(F32)
            mixed_ref[rows, :] = total.astype(BF)

        halves(h, body)

    def weights_ready(h, s):
        for j in range(1, NPOP):
            for c in exchange(j):
                c.wait_recv()
        shape_weights()

    def step_slot(h, t):
        step(t)
        outs[t].start()

    tasks = {
        "S": send_on, "P": project_slot, "F": finish, "D": down_slot,
        "R": send_back, "L": last, "X": weights_ready, "T": step_slot, "K": pack,
    }
    for at, word in enumerate(ORDER):
        tasks[word[0]]("AB".index(word[1]), int(word[2:]))
        if at == ROOTS:
            load_weights()

    ag_all = pltpu.make_async_remote_copy(
        src_ref=tok.at[pl.ds(0, OWN)], dst_ref=tok.at[pl.ds(0, OWN)], send_sem=ag_send, recv_sem=ag_recv.at[0, 0],
        device_id=near(0, 1), device_id_type=MESH,
    )
    rs_all = pltpu.make_async_remote_copy(
        src_ref=part.at[pl.ds(0, OWN)], dst_ref=rsr, send_sem=rs_send, recv_sem=rs_recv.at[0, 0],
        device_id=near(0, 1), device_id_type=MESH,
    )
    ag_all.wait_send()
    rs_all.wait_send()
    for j in range(1, NPOP):
        for c in exchange(j):
            c.wait_send()
    for c in outs:
        c.wait()


def per_device(tokens, norm_gain, gate_weight, up_weight, down_weight, gate_left, up_left, down_right,
               gate_right, up_right, down_left, fitness):
    vm = pltpu.VMEM
    dma = pltpu.SemaphoreType.DMA
    anywhere = pl.BlockSpec(memory_space=pl.ANY)
    mixed, gate_step, up_step, down_step = pl.pallas_call(
        kernel,
        out_shape=(
            pltpu.VMEM((ROWS, FB), BF),
            pltpu.VMEM((FFB, 512), BF),
            pltpu.VMEM((FFB, 512), BF),
            pltpu.VMEM((FFB, 512), BF),
        ),
        in_specs=[anywhere] * 12,
        out_specs=(pl.BlockSpec(memory_space=pltpu.VMEM),) * 4,
        scratch_shapes=[
            vm((32, ROWS, FB), BF),
            vm((FFB, D), BF),
            vm((FFB, D), BF),
            vm((512, D), BF),
            vm((ROWS, FFB), F32),
            vm((ROWS, FFB), F32),
            vm((ROWS, 64), F32),
            vm((ROWS, FB), F32),
            vm((ROWS, 512), BF),
            vm((32, ROWS, FB), BF),
            vm((31, ROWS, FB), BF),
            vm((4, 4, D), BF),
            vm((4, 4, D), BF),
            vm((4, 4, D), BF),
            vm((4, 4, FFB), BF),
            vm((4, 4, FFB), BF),
            vm((4, 4, FFB), BF),
            vm((16, D), F32),
            vm((16, 512), F32),
            vm((64, D), BF),
            vm((64, 512), BF),
            vm((64, 512), BF),
            vm((128, 512), BF),
            vm((48, D), BF),
            vm((48, 512), BF),
            vm((8, 128), F32),
            vm((8, 48, 512), BF),
            vm((8, 48, 512), BF),
            vm((8, 8, 128), F32),
            vm((32, FB), F32),
            vm((32, FB), F32),
            vm((1, 8), F32),
            vm((128, 128), F32),
            vm((512, 512), BF),
            vm((512, 512), BF),
            vm((512, 512), BF),
            dma((24,)),
            dma((9,)),
            dma((3,)),
            dma,
            dma((31, NCH)),
            dma,
            dma((31, NCH)),
            dma((8, 3)),
            dma((8, 3)),
        ],
        compiler_params=pltpu.CompilerParams(
            collective_id=0, has_side_effects=True, vmem_limit_bytes=56 << 20
        ),
        cost_estimate=pl.CostEstimate(flops=6_500_000_000, bytes_accessed=14_000_000, transcendentals=250_000),
        name="es_step",
    )(
        tokens, norm_gain.reshape(32, FB), gate_weight.T, up_weight.T, down_weight, gate_left, up_left, down_right,
        gate_right, up_right, down_left, fitness.reshape(1, 8),
    )
    mixed, gate_step, up_step, down_step = hand_over(mixed, gate_step, up_step, down_step)
    return mixed, gate_step.T, up_step.T, down_step


def move(a, b, c, d, a_out, b_out, c_out, d_out, sem):
    copies = [
        pltpu.make_async_copy(i, o, sem.at[n])
        for n, (i, o) in enumerate(((b, b_out), (c, c_out), (d, d_out), (a, a_out)))
    ]
    for c in copies:
        c.start()
    for c in copies:
        c.wait()


def hand_over(*arrays):
    anywhere = pl.BlockSpec(memory_space=pl.ANY)
    return pl.pallas_call(
        move,
        out_shape=tuple(jax.ShapeDtypeStruct(a.shape, a.dtype) for a in arrays),
        in_specs=[anywhere] * 4,
        out_specs=(anywhere,) * 4,
        scratch_shapes=[pltpu.SemaphoreType.DMA((4,))],
        compiler_params=pltpu.CompilerParams(vmem_limit_bytes=1 << 20),
        name="hand_over",
    )(*arrays)


def solution(mesh):
    in_specs = (
        P("pop", "mp"),
        P(),
        P(None, "mp"),
        P(None, "mp"),
        P("mp", None),
        P("pop", None, None),
        P("pop", None, None),
        P("pop", None, None),
        P("pop", None, "mp"),
        P("pop", None, "mp"),
        P("pop", None, "mp"),
        P("pop"),
    )
    out_specs = (P("pop", "mp"), P("pop", "mp"), P("pop", "mp"), P("mp", "pop"))
    return jax.shard_map(
        per_device, mesh=mesh, in_specs=in_specs, out_specs=out_specs, check_vma=False
    )
```

```python
import math

import jax
import jax.numpy as jnp
from jax import lax
from jax.experimental import pallas as pl
from jax.experimental.pallas import tpu as pltpu
from jax.sharding import PartitionSpec as P

MESH = pl.DeviceIdType.MESH
BF = jnp.bfloat16
F32 = jnp.float32

NX, NZ, NPOP = 4, 8, 8
ROWS, FB, FFB, D, FF = 512, 128, 464, 4096, 14848
NCH = 4
RC = ROWS // NCH
HALF = ROWS // 2
SLOTS = 8

OFFSET = (
    (2, 1), (3, 1), (1, 2), (1, 0), (1, 1), (2, 0), (0, 1), (3, 6), (3, 5), (3, 0), (3, 3), (2, 7),
    (0, 7), (3, 7), (0, 2), (0, 6), (1, 3), (0, 4), (2, 6), (1, 5), (1, 7), (0, 5), (0, 3), (1, 6),
    (1, 4), (2, 5), (3, 2), (2, 2), (2, 3), (3, 4), (2, 4),
    (0, 0),
)
GATHER = (
    (
        (0, 1, 4), (2, 1, 9), (2, 1, 4), (0, 1, 31), (0, 1, 6), (1, 1, 9), (2, 1, 31), (1, 1, 15),
        (1, 1, 21), (1, 1, 31), (1, 1, 22), (1, 1, 13), (3, 1, 31), (1, 1, 12), (2, 1, 6), (3, 1, 12),
        (0, 1, 22), (3, 1, 21), (0, 1, 23), (3, 1, 23), (3, 1, 3), (3, 1, 15), (2, 1, 14), (0, 1, 15),
        (3, 1, 19), (0, 1, 19), (2, 1, 1), (2, 1, 0), (1, 1, 10), (2, 1, 10), (3, 1, 25),
    ),
    (
        (0, 1, 4), (2, 1, 9), (2, 1, 4), (0, 1, 31), (0, 1, 6), (1, 1, 9), (2, 1, 31), (1, 1, 15),
        (1, 1, 21), (1, 1, 31), (1, 1, 22), (0, 1, 20), (3, 1, 31), (1, 1, 12), (2, 1, 6), (3, 1, 12),
        (0, 1, 22), (2, 1, 22), (1, 1, 7), (3, 1, 23), (3, 1, 3), (3, 1, 15), (2, 1, 14), (0, 1, 15),
        (3, 1, 19), (0, 1, 19), (2, 1, 1), (0, 1, 2), (1, 1, 10), (2, 1, 10), (3, 1, 25),
    ),
)
SCATTER = (
    (
        (0, 1, 4), (2, 1, 9), (2, 1, 4), (0, 1, 31), (0, 1, 6), (1, 1, 9), (2, 1, 31), (1, 1, 15),
        (1, 1, 21), (1, 1, 31), (1, 1, 22), (1, 1, 13), (3, 1, 31), (1, 1, 12), (2, 1, 6), (3, 1, 12),
        (0, 1, 22), (2, 1, 22), (0, 1, 23), (3, 1, 23), (3, 1, 3), (3, 1, 15), (2, 1, 14), (0, 1, 15),
        (3, 1, 19), (0, 1, 19), (2, 1, 1), (0, 1, 2), (1, 1, 10), (2, 1, 10), (3, 1, 25),
    ),
    (
        (0, 1, 4), (2, 1, 9), (2, 1, 4), (0, 1, 31), (0, 1, 6), (1, 1, 9), (2, 1, 31), (1, 1, 15),
        (1, 1, 21), (1, 1, 31), (1, 1, 22), (1, 1, 13), (3, 1, 31), (1, 1, 12), (2, 1, 6), (3, 1, 12),
        (0, 1, 22), (3, 1, 21), (0, 1, 23), (3, 1, 23), (3, 1, 3), (3, 1, 15), (2, 1, 14), (0, 1, 15),
        (3, 1, 19), (0, 1, 19), (2, 1, 1), (2, 1, 0), (1, 1, 10), (2, 1, 10), (3, 1, 25),
    ),
)
OWN = 31
CHILDREN = [[[c for c in range(OWN) if tree[c][2] == n] for n in range(32)] for tree in SCATTER]
GROUP = [list(range(4 * s, 4 * s + 4)) for s in range(SLOTS)]
REACH = sorted({(e[0] ^ turn, e[1]) for tree in GATHER + SCATTER for e in tree for turn in (0, 1)})

ORDER = (
    "SA12", "SB12", "SA6", "SB9", "SA3", "SB6", "SB3", "SA9", "KA0", "SA15", "SA13", "SA14", "SA4", "SB5",
    "SB15", "SB14", "SB4", "SA5", "SA1", "SA20", "SA23", "SA21", "SB13", "SA22", "SB23", "SB21", "SA7", "SB22",
    "SA2", "SA0", "SB7", "SB2", "SB1", "SA19", "SB0", "PA3", "SB20", "SA10", "SA16", "SB19", "SA17", "SA8",
    "SA26", "SA11", "SA25", "SA24", "PB1", "SA18", "SB10", "PB3", "SA27", "SA29", "PA1", "PA0", "SA28", "SB25",
    "SB16", "SB18", "SA30", "SB26", "SB11", "PB5", "SB27", "SB17", "PA2", "SB24", "SB8", "PA4", "SB29", "PA5",
    "PA6", "SB28", "SB30", "PB0", "PA7", "FA0", "DA4", "DA7", "RA17", "RA30", "RA16", "RA28", "DA2", "DA6",
    "RA8", "RA27", "RA29", "RA24", "RA11", "RA26", "PB2", "PB4", "RA18", "PB6", "PB7", "FB0", "DB7", "RB30",
    "RB29", "RB28", "DB4", "RA25", "DB6", "RB17", "DA3", "DA0", "RB27", "DA5", "RA10", "DB1", "RB16", "DB0",
    "DB2", "RB24", "RA2", "RB8", "XA0", "RB26", "RB25", "RB18", "RA19", "RB10", "RB11", "RA0", "DB5", "RB2",
    "RA21", "DA1", "RA1", "RA7", "DB3", "RB7", "RB0", "RB19", "RA22", "RA5", "RA23", "RB20", "TA2", "RB5",
    "RB22", "RB21", "RA20", "RB1", "RB23", "RA13", "RA4", "RA14", "RA15", "RB4", "RB14", "RB13", "RB15", "RA9",
    "RB9", "RA3", "RA6", "RA12", "RB3", "RB6", "RB12", "TA1", "TA0", "LA0", "LB0",
)
ROOTS = max(at for at in range(12) if ORDER[at][0] == "S" and GATHER["AB".index(ORDER[at][1])][int(ORDER[at][2:])][2] == OWN)


def nt(a, b):
    return lax.dot_general(a, b, (((1,), (1,)), ((), ())), preferred_element_type=F32)


def mm(a, b):
    return jnp.dot(a, b, preferred_element_type=F32)


def kernel(
    tok_h, gain_h, wg_h, wu_h, wd_h, gl_h, ul_h, dr_h, gr_h, ur_h, dl_h, fit_h,
    mixed_ref, gs_h, us_h, ds_h,
    tok, wg, wu, wd, accg, accu, accp, sq, hid, part, rsr,
    gl, ul, dr, gr, ur, dl, lf, rf, lx, rxg, rxu, dlx,
    lsend, rsend, fsend, lrecv, rrecv, frecv, gain, gainp, fit, wcol, gsb, usb, dsb,
    wsem, lsem, osem, ag_send, ag_recv, rs_send, rs_recv, x_send, x_recv,
):
    p = lax.axis_index("pop")
    m = lax.axis_index("mp")
    x, z = m // NZ, m % NZ

    def near(k, hops):
        if k < 2:
            return (p, ((x + (hops, NX - hops)[k]) % NX) * NZ + z)
        return (p, x * NZ + (z + (hops, NZ - hops)[k - 2]) % NZ)

    def source(n):
        dx, dz = OFFSET[n]
        return ((x + NX - dx) % NX) * NZ + (z + NZ - dz) % NZ

    def peer(j):
        return ((p + j) % NPOP, m)

    own = pltpu.make_async_copy(tok_h, tok.at[OWN], lsem.at[0])
    own.start()
    small = [
        pltpu.make_async_copy(a, b, lsem.at[1 + i])
        for i, (a, b) in enumerate(
            ((gl_h, gl), (ul_h, ul), (dr_h, dr), (gr_h, gr), (ur_h, ur), (dl_h, dl), (gain_h, gain), (fit_h, fit))
        )
    ]
    for c in small:
        c.start()

    bar = pltpu.get_barrier_semaphore()
    for k, hops in REACH:
        pl.semaphore_signal(bar, inc=1, device_id=near(k, hops), device_id_type=MESH)
    for j in range(1, NPOP):
        pl.semaphore_signal(bar, inc=1, device_id=peer(j), device_id_type=MESH)

    def wait_in(s):
        cols = pl.ds(s * 512, 512)
        pltpu.make_async_copy(wg_h.at[:, pl.ds(0, 512)], wg.at[:, cols], wsem.at[s]).wait()
        pltpu.make_async_copy(wu_h.at[:, pl.ds(0, 512)], wu.at[:, cols], wsem.at[8 + s]).wait()

    def wait_down(s):
        pltpu.make_async_copy(
            wd_h.at[:, pl.ds(0, 512)], wd.at[pl.ds(0, FFB), pl.ds(s * 512, 512)], wsem.at[16 + s]
        ).wait()

    def rows_of(i):
        return pl.ds(pl.multiple_of(i * RC, RC), RC)

    def ag(h, n, i):
        k, hops, parent = GATHER[h][n]
        return pltpu.make_async_remote_copy(
            src_ref=(tok_h if parent == OWN else tok.at[parent]).at[rows_of(i)], dst_ref=tok.at[n].at[rows_of(i)],
            send_sem=ag_send, recv_sem=ag_recv.at[n, i],
            device_id=near(k, hops), device_id_type=MESH,
        )

    def rs(h, n, i):
        k, hops, _ = SCATTER[h][n]
        return pltpu.make_async_remote_copy(
            src_ref=part.at[n].at[rows_of(i)], dst_ref=rsr.at[n].at[rows_of(i)],
            send_sem=rs_send, recv_sem=rs_recv.at[n, i],
            device_id=near(k ^ 1, hops), device_id_type=MESH,
        )

    def exchange(j):
        to = (p + j) % NPOP
        cols = pl.ds(pl.multiple_of(to * 512, 512), 512)
        return [
            pltpu.make_async_remote_copy(
                src_ref=a, dst_ref=b, send_sem=x_send.at[j, q], recv_sem=x_recv.at[j, q],
                device_id=peer(j), device_id_type=MESH,
            )
            for q, (a, b) in enumerate(
                ((fsend, frecv.at[j]), (rsend, rrecv.at[j]), (lsend.at[:, cols], lrecv.at[j]))
            )
        ]

    pl.semaphore_wait(bar, len(REACH) + NPOP - 1)

    def load_weights():
        for s in range(SLOTS):
            for n in GROUP[s]:
                cols = pl.ds(pl.multiple_of(source(n) * FB, FB), FB)
                to = pl.ds(n * FB, FB)
                pltpu.make_async_copy(wg_h.at[:, cols], wg.at[:, to], wsem.at[s]).start()
                pltpu.make_async_copy(wu_h.at[:, cols], wu.at[:, to], wsem.at[8 + s]).start()
        for s in reversed(range(SLOTS)):
            for n in GROUP[s]:
                cols = pl.ds(pl.multiple_of(source(n) * FB, FB), FB)
                pltpu.make_async_copy(
                    wd_h.at[:, cols], wd.at[pl.ds(0, FFB), pl.ds(n * FB, FB)], wsem.at[16 + s]
                ).start()

    def pack(h, s):
        own.wait()

        for c in small:
            c.wait()
        fsend[...] = jnp.zeros((8, 128), F32)
        fsend[0:1, 0:8] = fit[...]
        rf[...] = jnp.zeros((16, 512), F32)
        for t, ref in enumerate((gr, ur, dl)):
            for k in range(4):
                rf[4 * k : 4 * k + 4, 0:FFB] = ref[k].astype(F32)
            rsend[16 * t : 16 * t + 16, :] = rf[...].astype(BF)
        for t, ref in enumerate((gl, ul, dr)):
            for k in range(4):
                lf[4 * k : 4 * k + 4, :] = ref[k].astype(F32)
            lsend[16 * t : 16 * t + 16, :] = lf[...].astype(BF)
        for j in range(1, NPOP):
            for c in exchange(j):
                c.start()
        frecv[0] = fsend[...]
        rrecv[0] = rsend[...]
        lrecv[0] = lsend[:, pl.ds(pl.multiple_of(p * 512, 512), 512)]

        zero16 = jnp.zeros((16, 512), BF)
        rxg[...] = jnp.concatenate([rsend[0:16, :], rsend[0:16, :], zero16, zero16], axis=0)
        rxu[...] = jnp.concatenate([zero16, zero16, rsend[16:32, :], rsend[16:32, :]], axis=0)
        dlx[...] = jnp.concatenate([zero16] * 5 + [rsend[32:48, :], rsend[32:48, :], zero16], axis=0)
        for n in range(32):
            cols = pl.ds(pl.multiple_of(source(n) * FB, FB), FB)
            to = pl.ds(n * FB, FB)
            a, b, c = lsend[0:16, cols], lsend[16:32, cols], lsend[32:48, cols]
            lx[:, to] = jnp.concatenate([a, a, b, b], axis=0)
            wd[FFB:512, to] = jnp.concatenate([c, c, jnp.zeros((16, FB), BF)], axis=0)
            gainp[n : n + 1, :] = gain[pl.ds(source(n), 1), :]
        hid[:, 384:512] = jnp.zeros((ROWS, 128), BF)

    def project(s, h, first):
        rows = slice(h * HALF, h * HALF + HALF)
        blocks, square = [], None
        for n in GROUP[s]:
            t = tok[n, rows, :].astype(F32)
            square = t * t if square is None else square + t * t
            blocks.append((t * gainp[n : n + 1, :]).astype(BF))
        v = jnp.concatenate(blocks, axis=1)
        at = slice(s * 512, s * 512 + 512)
        g, u, q = nt(v, wg[:, at]), nt(v, wu[:, at]), nt(v, lx[:, at])
        if first:
            accg[rows, :], accu[rows, :], accp[rows, :], sq[rows, :] = g, u, q, square
        else:
            accg[rows, :] += g
            accu[rows, :] += u
            accp[rows, :] += q
            sq[rows, :] += square

    def weighting(h, lanes):
        row = lax.broadcasted_iota(jnp.int32, (HALF, lanes), 0) + h * HALF
        lane = lax.broadcasted_iota(jnp.int32, (HALF, lanes), 1)
        member = row // 64
        sign = (1 - 2 * (member % 2)).astype(F32)
        return jnp.where((lane % 16) // 4 == member // 2, sign, 0.0), lane

    def split(value, first):
        high = value.astype(BF).astype(F32)
        return jnp.where(first, high, value - high).astype(BF)

    def finish(h, s):
        rows = slice(h * HALF, h * HALF + HALF)
        scale = lax.rsqrt(jnp.sum(sq[rows, :], axis=1, keepdims=True) * (1.0 / D) + 1e-06)
        sign, lane = weighting(h, 64)
        coef = sign * (accp[rows, :] * scale) * (0.5 / math.sqrt(D))
        coef = split(coef, lane % 32 < 16)
        gate = accg[rows, :] * scale + mm(coef, rxg[:, 0:FFB])
        up = accu[rows, :] * scale + mm(coef, rxu[:, 0:FFB])
        hid[rows, 0:FFB] = (gate / (1.0 + jnp.exp(-gate)) * up).astype(BF)
        projected = nt(hid[rows, :], dlx[...])
        sign, lane = weighting(h, 128)
        coef = sign * projected * (0.5 / math.sqrt(FF))
        coef = split(coef, lane < 96)
        tail = hid[rows, 384:512]
        inside = (lane < 80).astype(F32)
        pert = ((lane >= 80) & (lane < 112)).astype(F32)
        hid[rows, 384:512] = jnp.where(
            inside > 0, tail.astype(F32), jnp.where(pert > 0, coef.astype(F32), 0.0)
        ).astype(BF)

    def down(s, h):
        rows = slice(h * HALF, h * HALF + HALF)
        y = mm(hid[rows, :], wd[:, s * 512 : s * 512 + 512])
        for q, n in enumerate(GROUP[s]):
            part[n, rows, :] = y[:, q * FB : (q + 1) * FB].astype(BF)

    def add_children(h, n, i):
        rows = rows_of(i)
        if CHILDREN[h][n]:
            total = part[n, rows, :].astype(F32)
            for c in CHILDREN[h][n]:
                rs(h, c, i).wait_recv()
                total = total + rsr[c, rows, :].astype(F32)
            return total
        return None

    def shape_weights():
        every = frecv[:, 0, :]
        lane = lax.broadcasted_iota(jnp.int32, (8, 128), 1)
        valid = lane < 8
        center = jnp.sum(jnp.where(valid, every, 0.0)) * (1.0 / 64)
        off = jnp.where(valid, every - center, 0.0)
        var = jnp.sum(off * off) * (1.0 / 64)
        shaped = off * lax.rsqrt(jnp.broadcast_to(var + 1e-05, (8, 128)))
        wide = jnp.broadcast_to(shaped[:, None, :], (8, 16, 128)).reshape(128, 128)
        row = lax.broadcasted_iota(jnp.int32, (128, 128), 0)
        lane = lax.broadcasted_iota(jnp.int32, (128, 128), 1)
        k = (row % 16) // 4
        pick = jnp.where(lane == 2 * k, 1.0, jnp.where(lane == 2 * k + 1, -1.0, 0.0))
        col = jnp.sum(wide * pick, axis=1, keepdims=True) * (1.0 / math.sqrt(128))
        wcol[...] = jnp.broadcast_to(col, (128, 128))

    def step(t):
        take = pl.ds(16 * t, 16)
        left = rrecv[:, take, :].reshape(128, 512).T
        right = lrecv[:, take, :].reshape(128, 512).astype(F32) * jnp.concatenate([wcol[...]] * 4, axis=1)
        high = right.astype(BF)
        low = (right - high.astype(F32)).astype(BF)
        out = mm(jnp.concatenate([left, left], axis=1), jnp.concatenate([high, low], axis=0))
        (gsb, usb, dsb)[t][...] = out.astype(BF)

    outs = [
        pltpu.make_async_copy(gsb.at[pl.ds(0, FFB)], gs_h, osem.at[0]),
        pltpu.make_async_copy(usb.at[pl.ds(0, FFB)], us_h, osem.at[1]),
        pltpu.make_async_copy(dsb.at[pl.ds(0, FFB)], ds_h, osem.at[2]),
    ]

    seen, ready_in, ready_down, begun = set(), set(), set(), set()

    def halves(h, body):
        def run(c, carry):
            body(2 * h + c)
            return carry

        lax.fori_loop(0, 2, run, 0)

    def arrive(h, blocks):
        new = [n for n in blocks if n != OWN and (h, n) not in seen]
        seen.update((h, n) for n in new)
        return new

    def send_on(h, n):
        new = arrive(h, [GATHER[h][n][2]])

        def body(i):
            for q in new:
                ag(h, q, i).wait_recv()
            ag(h, n, i).start()

        halves(h, body)

    def project_slot(h, s):
        if s not in ready_in:
            ready_in.add(s)
            wait_in(s)
        new, first = arrive(h, GROUP[s]), h not in begun
        begun.add(h)

        def body(i):
            for n in new:
                ag(h, n, i).wait_recv()

        halves(h, body)
        project(s, h, first)

    def down_slot(h, s):
        if s not in ready_down:
            ready_down.add(s)
            wait_down(s)
        down(s, h)

    def send_back(h, n):
        def body(i):
            total = add_children(h, n, i)
            if total is not None:
                part[n, rows_of(i), :] = total.astype(BF)
            rs(h, n, i).start()

        halves(h, body)

    def last(h, s):
        def body(i):
            rows = rows_of(i)
            total = add_children(h, OWN, i) + tok[OWN, rows, :].astype(F32)
            mixed_ref[rows, :] = total.astype(BF)

        halves(h, body)

    def weights_ready(h, s):
        for j in range(1, NPOP):
            for c in exchange(j):
                c.wait_recv()
        shape_weights()

    def step_slot(h, t):
        step(t)
        outs[t].start()

    tasks = {
        "S": send_on, "P": project_slot, "F": finish, "D": down_slot,
        "R": send_back, "L": last, "X": weights_ready, "T": step_slot, "K": pack,
    }
    for at, word in enumerate(ORDER):
        tasks[word[0]]("AB".index(word[1]), int(word[2:]))
        if at == ROOTS:
            load_weights()

    ag_all = pltpu.make_async_remote_copy(
        src_ref=tok.at[pl.ds(0, OWN)], dst_ref=tok.at[pl.ds(0, OWN)], send_sem=ag_send, recv_sem=ag_recv.at[0, 0],
        device_id=near(0, 1), device_id_type=MESH,
    )
    rs_all = pltpu.make_async_remote_copy(
        src_ref=part.at[pl.ds(0, OWN)], dst_ref=rsr, send_sem=rs_send, recv_sem=rs_recv.at[0, 0],
        device_id=near(0, 1), device_id_type=MESH,
    )
    ag_all.wait_send()
    rs_all.wait_send()
    for j in range(1, NPOP):
        for c in exchange(j):
            c.wait_send()
    for c in outs:
        c.wait()


def per_device(tokens, norm_gain, gate_weight, up_weight, down_weight, gate_left, up_left, down_right,
               gate_right, up_right, down_left, fitness):
    vm = pltpu.VMEM
    dma = pltpu.SemaphoreType.DMA
    anywhere = pl.BlockSpec(memory_space=pl.ANY)
    mixed, gate_step, up_step, down_step = pl.pallas_call(
        kernel,
        out_shape=(
            pltpu.VMEM((ROWS, FB), BF),
            pltpu.VMEM((FFB, 512), BF),
            pltpu.VMEM((FFB, 512), BF),
            pltpu.VMEM((FFB, 512), BF),
        ),
        in_specs=[anywhere] * 12,
        out_specs=(pl.BlockSpec(memory_space=pltpu.VMEM),) * 4,
        scratch_shapes=[
            vm((32, ROWS, FB), BF),
            vm((FFB, D), BF),
            vm((FFB, D), BF),
            vm((512, D), BF),
            vm((ROWS, FFB), F32),
            vm((ROWS, FFB), F32),
            vm((ROWS, 64), F32),
            vm((ROWS, FB), F32),
            vm((ROWS, 512), BF),
            vm((32, ROWS, FB), BF),
            vm((31, ROWS, FB), BF),
            vm((4, 4, D), BF),
            vm((4, 4, D), BF),
            vm((4, 4, D), BF),
            vm((4, 4, FFB), BF),
            vm((4, 4, FFB), BF),
            vm((4, 4, FFB), BF),
            vm((16, D), F32),
            vm((16, 512), F32),
            vm((64, D), BF),
            vm((64, 512), BF),
            vm((64, 512), BF),
            vm((128, 512), BF),
            vm((48, D), BF),
            vm((48, 512), BF),
            vm((8, 128), F32),
            vm((8, 48, 512), BF),
            vm((8, 48, 512), BF),
            vm((8, 8, 128), F32),
            vm((32, FB), F32),
            vm((32, FB), F32),
            vm((1, 8), F32),
            vm((128, 128), F32),
            vm((512, 512), BF),
            vm((512, 512), BF),
            vm((512, 512), BF),
            dma((24,)),
            dma((9,)),
            dma((3,)),
            dma,
            dma((31, NCH)),
            dma,
            dma((31, NCH)),
            dma((8, 3)),
            dma((8, 3)),
        ],
        compiler_params=pltpu.CompilerParams(
            collective_id=0, has_side_effects=True, vmem_limit_bytes=56 << 20
        ),
        cost_estimate=pl.CostEstimate(flops=6_500_000_000, bytes_accessed=14_000_000, transcendentals=250_000),
        name="es_step",
    )(
        tokens, norm_gain.reshape(32, FB), gate_weight.T, up_weight.T, down_weight, gate_left, up_left, down_right,
        gate_right, up_right, down_left, fitness.reshape(1, 8),
    )
    mixed, gate_step, up_step, down_step = hand_over(mixed, gate_step, up_step, down_step)
    return mixed, gate_step.T, up_step.T, down_step


def move(a, b, c, d, a_out, b_out, c_out, d_out, sem):
    copies = [
        pltpu.make_async_copy(i, o, sem.at[n])
        for n, (i, o) in enumerate(((b, b_out), (c, c_out), (d, d_out), (a, a_out)))
    ]
    for c in copies:
        c.start()
    for c in copies:
        c.wait()


def hand_over(*arrays):
    anywhere = pl.BlockSpec(memory_space=pl.ANY)
    return pl.pallas_call(
        move,
        out_shape=tuple(jax.ShapeDtypeStruct(a.shape, a.dtype) for a in arrays),
        in_specs=[anywhere] * 4,
        out_specs=(anywhere,) * 4,
        scratch_shapes=[pltpu.SemaphoreType.DMA((4,))],
        compiler_params=pltpu.CompilerParams(vmem_limit_bytes=1 << 20),
        name="hand_over",
    )(*arrays)


def solution(mesh):
    in_specs = (
        P("pop", "mp"),
        P(),
        P(None, "mp"),
        P(None, "mp"),
        P("mp", None),
        P("pop", None, None),
        P("pop", None, None),
        P("pop", None, None),
        P("pop", None, "mp"),
        P("pop", None, "mp"),
        P("pop", None, "mp"),
        P("pop"),
    )
    out_specs = (P("pop", "mp"), P("pop", "mp"), P("pop", "mp"), P("mp", "pop"))
    return jax.shard_map(
        per_device, mesh=mesh, in_specs=in_specs, out_specs=out_specs, check_vma=False
    )
```
